32 devices in a mesh: groups: 2 (over x), section: 2 (over core), tp: 8 (over z, y).
Axes of the slice: x: 2, y: 2, z: 4, core: 2. Of those that a mesh axis runs over, the one named last changes fastest.
Arguments:
- hidden: bfloat16 [2, 256, 8192], P('section', 'groups', 'tp'), parts along dimension 1, may hold values from -6 to 6
- norm_gain: float32 [2, 8192], P('section'), may hold values from 0.1 to 1.9
- w_query: bfloat16 [2, 8192, 8192], P('section', None, 'tp'), may hold values from -0.0625 to 0.0625
- key_value_weight: bfloat16 [2, 8192, 2048], P('section', None, 'tp'), may hold values from -0.0625 to 0.0625
- w_out: bfloat16 [2, 8192, 8192], P('section', 'tp'), may hold values from -0.875 to 0.875
- cache_pages: bfloat16 [2, 16384, 2048], P('section', ('groups', 'tp')), parts along dimension 1, may hold values from -260 to 260
- prefix_len: int32 [2, 2], P('section', 'groups'), parts along dimension 1, may hold values from 4096 to 8192, as said below
- page_owner: int32 [2, 32], P('section', 'groups'), parts along dimension 1, may hold values from 0 to 7, as said below
Outputs:
- handed: bfloat16 [2, 256, 8192], P('section', 'groups', 'tp'), parts along dimension 1
- pages_out: bfloat16 [2, 8, 8, 8, 2048], P('section', 'tp', 'groups'), parts along dimension 2
The draws below stay inside these ranges and needn't reach their ends.
There are 2 independent parts, one for each index of `groups`. The reference program is written for one: setup_inputs(seed, part) draws one part's arguments, and reference() takes and returns one part's arrays. A program takes and returns all parts, laid end to end along the dimension named above; an argument that names none is the same for every part. Nothing has to cross between parts.
Inputs may be any that keep to these rules, and one draw needn't show every extreme that they name: `page_owner`: for each section at most 4 pages share an owner, and some owner has exactly 4. prefix_len of the first section is 8192.
All inputs are finite; a program needn't handle non-finite values.
Results may differ from the reference program's by a relative error of at most 0.028.
Values may be sent and summed in bfloat16 or wider, within the bound.
A program may use at most 128 MiB of HBM per device.

```python
import jax
import jax.numpy as jnp
from jax import lax

MODEL_WIDTH = 8192
QUERY_HEADS = 64
KEY_VALUE_HEADS = 8
HEAD_SIZE = 128
SPAN_TOKENS = 128
PAGE = 8
MOST = 4
NPAGE = 16
CACHED_SLOTS = 8192
RELAY_SECTIONS = 2
N_TP = 8


def draw_page_owner(key, part):
    section_rows = []
    for section_index in range(RELAY_SECTIONS):
        section_key = jax.random.fold_in(key, 11 + section_index)
        owner_perm = jax.random.permutation(jax.random.fold_in(section_key, 1), N_TP).astype(jnp.int32)
        page_order = jax.random.permutation(jax.random.fold_in(section_key, 2), NPAGE).astype(jnp.int32)
        slot_index = jnp.arange(NPAGE, dtype=jnp.int32)
        others = 1 + jnp.mod(slot_index - MOST + (N_TP - 1) * NPAGE, N_TP - 1)
        chosen = jnp.where(slot_index < MOST, 0, others)
        slot_owner = owner_perm[chosen]
        owners = jnp.zeros((NPAGE,), jnp.int32).at[page_order].set(slot_owner)
        section_rows.append(owners)
    return jnp.stack(section_rows).astype(jnp.int32)


def draw_prefix_len(key, part):
    later = jax.random.randint(jax.random.fold_in(key, 5), (RELAY_SECTIONS, 1), CACHED_SLOTS // 2, CACHED_SLOTS - SPAN_TOKENS + 1)
    first_row = (jnp.arange(RELAY_SECTIONS, dtype=jnp.int32) == 0)[:, None]
    return jnp.where(first_row, CACHED_SLOTS, later).astype(jnp.int32)


def draw_cache_pages(key, part):
    sampled_inputs = jnp.clip(jax.random.normal(jax.random.fold_in(key, 21), (RELAY_SECTIONS, CACHED_SLOTS, 2 * KEY_VALUE_HEADS * HEAD_SIZE), jnp.float32), -4.0, 4.0) * 1.5
    return sampled_inputs.astype(jnp.bfloat16)


def strengthened(entries, key, source, target, parts, factor):
    def block_of(dim):
        return (jnp.arange(entries.shape[dim]) // (entries.shape[dim] // parts)).reshape((-1,) + (1,) * (entries.ndim - 1 - dim))

    one_side = jax.random.permutation(key, parts)[block_of(target)]
    other_side = (block_of(target) + parts // 2) % parts
    return jnp.where((block_of(source) == one_side) | (block_of(source) == other_side), factor * entries, entries)


def steps_of(rng, dims, shards, least, largest):
    gain, own = 1.0, jax.random.fold_in(rng, 6)
    for axis_at, shards_of in shards:
        heights = jnp.exp(jax.random.uniform(jax.random.fold_in(own, axis_at), (shards_of,), jnp.float32, least / len(shards), largest / len(shards)))
        gain = gain * jnp.repeat(heights, dims[axis_at] // shards_of).reshape([-1 if axis == axis_at else 1 for axis in range(len(dims))])
    return gain


def normal_values(own_key, dims, width, limit, pieces=(), held_as=jnp.bfloat16):
    gain = steps_of(own_key, dims, pieces, -0.22, 0.18) if pieces else 1.0
    result = jax.random.normal(own_key, dims, jnp.float32) * width * gain
    return jnp.minimum(jnp.maximum(result, -limit), limit).astype(held_as)


def noise_with(key, shape, spread, limit, cuts, heavy, held_as=jnp.bfloat16):
    entries = spread * jax.random.normal(key, shape, jnp.float32)
    if cuts:
        entries = entries * steps_of(key, shape, cuts, -0.22, 0.18)
    return jnp.clip(strengthened(entries, jax.random.fold_in(key, 3), *heavy), -limit, limit).astype(held_as)


def setup_inputs(seed: int = 0, part: int = 0) -> dict:
    splits = jax.random.split(jax.random.key(seed), 9)
    own_keys = jax.random.split(jax.random.fold_in(splits[8], part), 9)
    hidden = normal_values(own_keys[0], (RELAY_SECTIONS, SPAN_TOKENS, MODEL_WIDTH), 1.0, 6.0, ((0, 2), (2, 8)))
    norm_gain = jnp.clip(1.0 + 0.18 * jax.random.normal(splits[1], (RELAY_SECTIONS, MODEL_WIDTH), jnp.float32), 0.1, 1.9)
    w_query = normal_values(splits[2], (RELAY_SECTIONS, MODEL_WIDTH, QUERY_HEADS * HEAD_SIZE), MODEL_WIDTH ** -0.5, 0.0625, ((0, 2), (2, 8)))
    key_value_weight = normal_values(splits[3], (RELAY_SECTIONS, MODEL_WIDTH, 2 * KEY_VALUE_HEADS * HEAD_SIZE), MODEL_WIDTH ** -0.5, 0.0625, ((0, 2), (2, 8)))
    w_out = noise_with(splits[4], (RELAY_SECTIONS, QUERY_HEADS * HEAD_SIZE, MODEL_WIDTH), 0.1, 0.875, ((0, 2), (1, 8)), (1, 2, 8, 2.0))
    cache_pages = draw_cache_pages(jax.random.fold_in(jax.random.fold_in(splits[8], part), 71), part)
    prefix_len = draw_prefix_len(jax.random.fold_in(jax.random.fold_in(splits[8], part), 71), part)
    page_owner = draw_page_owner(jax.random.fold_in(jax.random.fold_in(splits[8], part), 71), part)
    return dict(hidden=hidden, norm_gain=norm_gain, w_query=w_query, key_value_weight=key_value_weight, w_out=w_out, cache_pages=cache_pages, prefix_len=prefix_len, page_owner=page_owner)


ROPE_BASE = 500000.0

def apply_rotary(values, token_places):
    head_width = values.shape[-1]
    half_width = head_width // 2
    inv_freq = ROPE_BASE ** (-jnp.arange(half_width, dtype=jnp.float32) * (2.0 / head_width))
    angles = token_places.astype(jnp.float32)[:, None] * inv_freq[None, :]
    cosine = jnp.cos(angles)[:, None, :]
    sine_part = jnp.sin(angles)[:, None, :]
    first_half = values[..., :half_width]
    second_half = values[..., half_width:]
    return jnp.concatenate([first_half * cosine - second_half * sine_part, second_half * cosine + first_half * sine_part], axis=-1)

def rotate_fresh(new_key_value, token_places):
    key_column_count = KEY_VALUE_HEADS * HEAD_SIZE
    rotary_output = apply_rotary(new_key_value[:, :key_column_count].astype(jnp.float32).reshape(-1, KEY_VALUE_HEADS, HEAD_SIZE), token_places)
    return jnp.concatenate([rotary_output.reshape(-1, key_column_count).astype(jnp.bfloat16), new_key_value[:, key_column_count:]], axis=1)

def reference(hidden, norm_gain, w_query, key_value_weight, w_out, cache_pages, prefix_len, page_owner):
    query_group_width = QUERY_HEADS // KEY_VALUE_HEADS
    key_column_count = KEY_VALUE_HEADS * HEAD_SIZE
    updated_all = []
    pages_all = []
    for section_index in range(RELAY_SECTIONS):
        rows_f32 = hidden[section_index].astype(jnp.float32)
        normed = (rows_f32 * lax.rsqrt(lax.optimization_barrier(jnp.mean(rows_f32 * rows_f32, axis=1, keepdims=True)) + 1e-05) * norm_gain[section_index][None, :]).astype(jnp.bfloat16)
        cached_len = prefix_len[section_index, 0]
        token_places = cached_len + jnp.arange(SPAN_TOKENS, dtype=jnp.int32)
        query_f32 = jnp.dot(normed, w_query[section_index], preferred_element_type=jnp.float32).reshape(SPAN_TOKENS, QUERY_HEADS, HEAD_SIZE)
        queries = apply_rotary(query_f32, token_places).astype(jnp.bfloat16)
        new_key_value = jnp.dot(normed, key_value_weight[section_index], preferred_element_type=jnp.float32).astype(jnp.bfloat16)
        fresh_rot = rotate_fresh(new_key_value, token_places)
        cached = cache_pages[section_index]
        all_keys = jnp.concatenate([cached[:, :key_column_count], fresh_rot[:, :key_column_count]], axis=0)
        all_values = jnp.concatenate([cached[:, key_column_count:], fresh_rot[:, key_column_count:]], axis=0)
        token_index = jnp.arange(SPAN_TOKENS, dtype=jnp.int32)
        cache_mask = jnp.broadcast_to((jnp.arange(CACHED_SLOTS, dtype=jnp.int32) < cached_len)[None, :], (SPAN_TOKENS, CACHED_SLOTS))
        fresh_mask = token_index[None, :] <= token_index[:, None]
        visible_key_mask = jnp.concatenate([cache_mask, fresh_mask], axis=1)

        def split_by_head(head_index):
            kv_head = head_index // query_group_width
            one_query = lax.dynamic_index_in_dim(queries, head_index, 1, keepdims=False)
            head_keys = lax.dynamic_slice_in_dim(all_keys, kv_head * HEAD_SIZE, HEAD_SIZE, 1)
            head_values = lax.dynamic_slice_in_dim(all_values, kv_head * HEAD_SIZE, HEAD_SIZE, 1)
            scores = jnp.dot(one_query, head_keys.T, preferred_element_type=jnp.float32) * HEAD_SIZE ** (-0.5)
            scores = jnp.where(visible_key_mask, scores, -jnp.inf)
            top_score = lax.optimization_barrier(jnp.max(scores, axis=1, keepdims=True))
            weights = jnp.exp(scores - top_score)
            denominator = lax.optimization_barrier(jnp.sum(weights, axis=1, keepdims=True))
            summed = jnp.dot(weights.astype(jnp.bfloat16), head_values, preferred_element_type=jnp.float32)
            return summed / denominator
        heads_out = lax.map(split_by_head, jnp.arange(QUERY_HEADS, dtype=jnp.int32))
        attended = jnp.transpose(heads_out, (1, 0, 2)).reshape(SPAN_TOKENS, QUERY_HEADS * HEAD_SIZE).astype(jnp.bfloat16)
        block_out = jnp.dot(attended, w_out[section_index], preferred_element_type=jnp.float32)
        updated_all.append((rows_f32 + block_out).astype(jnp.bfloat16))
        owners = page_owner[section_index]
        page_index = jnp.arange(NPAGE, dtype=jnp.int32)
        same_owner = owners[:, None] == owners[None, :]
        page_rank = lax.optimization_barrier(jnp.sum((same_owner & (page_index[None, :] < page_index[:, None])).astype(jnp.int32), axis=1))
        owner_index = jnp.arange(N_TP, dtype=jnp.int32)
        slot_index = jnp.arange(MOST, dtype=jnp.int32)
        matched = (owners[None, None, :] == owner_index[:, None, None]) & (page_rank[None, None, :] == slot_index[None, :, None])
        flat_pages = fresh_rot.reshape(NPAGE, PAGE * 2 * key_column_count).astype(jnp.float32)
        placed = jnp.einsum('osp,pf->osf', matched.astype(jnp.float32), flat_pages)
        pages_all.append(placed.astype(jnp.bfloat16).reshape(N_TP, MOST, PAGE, 2 * key_column_count))
    handed = jnp.roll(jnp.stack(updated_all), 1, axis=0)
    return (handed, jnp.stack(pages_all))
```

```python
import functools

import jax
import jax.numpy as jnp
import numpy as np
from jax import lax
from jax.experimental import pallas as pl
from jax.experimental.pallas import tpu as pltpu
from jax.sharding import PartitionSpec as P

QUERY_HEADS = 64
KEY_VALUE_HEADS = 8
HEAD_SIZE = 128
SPAN_TOKENS = 128
PAGE = 8
MOST = 4
NPAGE = 16


ROPE_BASE = 500000.0
NEG_FILL = -1e30


def passed_along(array, axis, by):
    length = lax.axis_size(axis)
    return lax.ppermute(array, axis, [(i, (i + by) % length) for i in range(length)])


def apply_rotary(values, token_places):
    head_width = values.shape[-1]
    half_width = head_width // 2
    inv_freq = ROPE_BASE ** (-jnp.arange(half_width, dtype=jnp.float32) * (2.0 / head_width))
    angles = token_places.astype(jnp.float32)[:, None] * inv_freq[None, :]
    cosine = jnp.cos(angles)[:, None, :]
    sine_part = jnp.sin(angles)[:, None, :]
    first_half = values[..., :half_width]
    second_half = values[..., half_width:]
    return jnp.concatenate(
        [
            first_half * cosine - second_half * sine_part,
            second_half * cosine + first_half * sine_part,
        ],
        axis=-1,
    )


def rotate_fresh(new_key_value, token_places):
    key_column_count = KEY_VALUE_HEADS * HEAD_SIZE
    rotary_output = apply_rotary(
        new_key_value[:, :key_column_count]
        .astype(jnp.float32)
        .reshape(-1, KEY_VALUE_HEADS, HEAD_SIZE),
        token_places,
    )
    return jnp.concatenate(
        [
            rotary_output.reshape(-1, key_column_count).astype(jnp.bfloat16),
            new_key_value[:, key_column_count:],
        ],
        axis=1,
    )


def fresh_pages(fresh_rot, owners, my_index):
    page_index = jnp.arange(NPAGE, dtype=jnp.int32)
    same_owner = owners[:, None] == owners[None, :]
    earlier = page_index[None, :] < page_index[:, None]
    page_rank = jnp.sum((same_owner & earlier).astype(jnp.int32), axis=1)
    slot_index = jnp.arange(MOST, dtype=jnp.int32)
    matched = (owners[None, :] == my_index) & (page_rank[None, :] == slot_index[:, None])
    flat_pages = fresh_rot.reshape(NPAGE, PAGE * fresh_rot.shape[1])
    picked = jnp.dot(
        matched.astype(jnp.bfloat16), flat_pages, preferred_element_type=jnp.float32
    ).astype(jnp.bfloat16)
    slot_page = jnp.sum(jnp.where(matched, page_index[None, :], 0), axis=1)
    slot_live = jnp.any(matched, axis=1)
    return (picked, slot_page, slot_live)


def on_device_plain(
    hidden, norm_gain, w_query, key_value_weight, w_out, cache_pages, prefix_len, page_owner
):
    tp_size = lax.axis_size("tp")
    my_index = lax.axis_index("tp")
    heads_here = QUERY_HEADS // tp_size
    query_group_width = QUERY_HEADS // KEY_VALUE_HEADS
    key_column_count = KEY_VALUE_HEADS * HEAD_SIZE
    own_rows = hidden[0]
    full_rows = lax.all_gather(own_rows, "tp", axis=1, tiled=True)
    rows_f32 = full_rows.astype(jnp.float32)
    normed = (
        rows_f32
        * lax.rsqrt(jnp.mean(rows_f32 * rows_f32, axis=1, keepdims=True) + 1e-05)
        * norm_gain[0][None, :]
    ).astype(jnp.bfloat16)
    cached_len = prefix_len[0, 0]
    token_index = jnp.arange(SPAN_TOKENS, dtype=jnp.int32)
    token_places = cached_len + token_index
    query_f32 = jnp.dot(normed, w_query[0], preferred_element_type=jnp.float32).reshape(
        SPAN_TOKENS, heads_here, HEAD_SIZE
    )
    queries = (
        apply_rotary(query_f32, token_places)
        .astype(jnp.bfloat16)
        .reshape(SPAN_TOKENS, heads_here * HEAD_SIZE)
    )
    fresh_part = jnp.dot(normed, key_value_weight[0], preferred_element_type=jnp.float32).astype(
        jnp.bfloat16
    )
    cached = cache_pages[0]
    slots_here = cached.shape[0]
    head_table = np.arange(tp_size) * heads_here // query_group_width
    by_head = jnp.transpose(
        cached.reshape(slots_here, 2, KEY_VALUE_HEADS, HEAD_SIZE), (2, 0, 1, 3)
    ).reshape(KEY_VALUE_HEADS, slots_here, 2 * HEAD_SIZE)
    outgoing = jnp.stack([by_head[int(h)] for h in head_table])
    arrived = lax.all_to_all(outgoing, "tp", split_axis=0, concat_axis=0, tiled=True)
    fresh_all = lax.all_gather(fresh_part, "tp", axis=1, tiled=True)
    fresh_rot = rotate_fresh(fresh_all, token_places)
    picked, slot_page, slot_live = fresh_pages(fresh_rot, page_owner[0], my_index)
    kv_head = my_index * heads_here // query_group_width
    local_key_rows = lax.dynamic_slice_in_dim(fresh_rot, kv_head * HEAD_SIZE, HEAD_SIZE, 1)
    local_value_rows = lax.dynamic_slice_in_dim(
        fresh_rot, key_column_count + kv_head * HEAD_SIZE, HEAD_SIZE, 1
    )
    all_keys = jnp.concatenate(
        [arrived[:, :, :HEAD_SIZE].reshape(tp_size * slots_here, HEAD_SIZE), local_key_rows], axis=0
    )
    all_values = jnp.concatenate(
        [arrived[:, :, HEAD_SIZE:].reshape(tp_size * slots_here, HEAD_SIZE), local_value_rows],
        axis=0,
    )
    cache_mask = jnp.broadcast_to(
        (jnp.arange(tp_size * slots_here, dtype=jnp.int32) < cached_len)[None, :],
        (SPAN_TOKENS, tp_size * slots_here),
    )
    fresh_mask = token_index[None, :] <= token_index[:, None]
    visible_key_mask = jnp.concatenate([cache_mask, fresh_mask], axis=1)
    head_queries = queries.reshape(SPAN_TOKENS, heads_here, HEAD_SIZE)

    def per_query(head_slot):
        one_head = lax.dynamic_index_in_dim(head_queries, head_slot, 1, keepdims=False)
        scores = jnp.einsum(
            "td,kd->tk", one_head, all_keys, preferred_element_type=jnp.float32
        ) * HEAD_SIZE ** (-0.5)
        scores = jnp.where(visible_key_mask, scores, NEG_FILL)
        top_score = jnp.max(scores, axis=1, keepdims=True)
        weights = jnp.exp(scores - top_score)
        denominator = jnp.sum(weights, axis=1, keepdims=True)
        summed = jnp.dot(
            weights.astype(jnp.bfloat16), all_values, preferred_element_type=jnp.float32
        )
        return summed / denominator

    outputs = lax.map(per_query, jnp.arange(heads_here, dtype=jnp.int32))
    attended = (
        jnp.transpose(outputs, (1, 0, 2))
        .reshape(SPAN_TOKENS, heads_here * HEAD_SIZE)
        .astype(jnp.bfloat16)
    )
    out_weight = w_out[0]
    block_share = lax.psum_scatter(
        lax.dot_general(
            out_weight, attended, (((0,), (1,)), ((), ())), preferred_element_type=jnp.float32
        ).astype(jnp.bfloat16),
        "tp",
        scatter_dimension=0,
        tiled=True,
    ).astype(jnp.float32)
    updated = (own_rows.astype(jnp.float32) + block_share.T).astype(jnp.bfloat16)
    handed = passed_along(updated, "section", 1)
    return (handed[None], picked.reshape(1, 1, MOST, PAGE, 2 * key_column_count))


LOG2E = 1.4426950408889634
VMEM_BYTES = 60 * 1024 * 1024
ANY = pl.BlockSpec(memory_space=pl.ANY)
VMEM = pl.BlockSpec(memory_space=pltpu.VMEM)


def layer_kernel(
    n, sections, heads_here,
    own_ref, gain_ref, cos_ref, sin_ref, bias_ref, wq_hbm, wkv_hbm, wo_hbm, cache_hbm,
    handed_ref, fresh_ref,
    wq, wkv, wo, cache, vt, hbuf, acc, sumsq, qbuf, obuf, mlbuf, own_o, own_ml, kvbuf, att,
    rbuf, upd, landed,
    w_sem, h_send, h_recv, q_send, q_recv, kv_send, kv_recv, o_send, o_recv, ml_send, ml_recv,
    r_send, r_recv, x_send, x_recv,
):
    f32, bf16 = jnp.float32, jnp.bfloat16
    tokens, width = own_ref.shape
    half = width // 2
    half_heads = heads_here // 2
    q_cols = heads_here * HEAD_SIZE
    kv_cols = wkv.shape[1]
    kv_half = kv_cols // 2
    key_cols = KEY_VALUE_HEADS * HEAD_SIZE
    rows = half_heads * tokens
    group = QUERY_HEADS // KEY_VALUE_HEADS

    me = lax.axis_index("tp")
    z, y = lax.div(me, 2), lax.rem(me, 2)
    place = y * (n - 1 - z) + (1 - y) * z

    def at_place(p):
        p = lax.rem(p + 2 * n, n)
        c = lax.div(p, n // 2)
        return (1 - c) * (2 * p) + c * (2 * (n - 1 - p) + 1)

    to = (at_place(place + 1), at_place(place - 1))

    def owner_at(d, s):
        return at_place(place - s) if d == 0 else at_place(place + s)

    def send(src, dst, ssem, rsem, d):
        return pltpu.make_async_remote_copy(
            src_ref=src, dst_ref=dst, send_sem=ssem, recv_sem=rsem,
            device_id={"tp": to[d]}, device_id_type=pl.DeviceIdType.MESH,
        )

    loads = [
        pltpu.make_async_copy(src, dst, w_sem.at[i])
        for i, (src, dst) in enumerate(
            ((wq_hbm, wq), (wkv_hbm, wkv), (cache_hbm, cache), (wo_hbm, wo))
        )
    ]
    loads[0].start()
    loads[1].start()

    sec = lax.axis_index("section")
    sec_next = lax.rem(sec + 1, sections)
    sec_prev = lax.rem(sec + sections - 1, sections)
    barrier = pltpu.get_barrier_semaphore()
    for d in range(2):
        pl.semaphore_signal(
            barrier, inc=1, device_id={"tp": to[d]}, device_id_type=pl.DeviceIdType.MESH
        )
    pl.semaphore_signal(
        barrier, inc=1, device_id={"section": sec_prev}, device_id_type=pl.DeviceIdType.MESH
    )
    for d in range(2):
        hbuf[d, 0] = own_ref[:, d * half : (d + 1) * half]
    acc[...] = jnp.zeros_like(acc)
    sumsq[...] = jnp.zeros_like(sumsq)
    pl.semaphore_wait(barrier, 3)

    def h_copy(d, s):
        return send(
            hbuf.at[d, s], hbuf.at[d, s + 1], h_send.at[d, s], h_recv.at[d, s + 1], d
        )

    def h_arrival(d, s):
        return send(hbuf.at[d, s - 1], hbuf.at[d, s], h_send.at[d, s], h_recv.at[d, s], d)

    def project(s, carry):
        for d in range(2):

            @pl.when(s > 0)
            def _():
                h_arrival(d, s).wait_recv()

            @pl.when(s < n - 1)
            def _():
                h_copy(d, s).start()

        @pl.when(s == 0)
        def _():
            loads[0].wait()
            loads[1].wait()
            loads[2].start()
            loads[3].start()

        for d in range(2):
            first = pl.multiple_of(owner_at(d, s) * width + d * half, 128)
            part = hbuf[d, s].astype(f32)
            sumsq[...] += jnp.sum(part * part, axis=1, keepdims=True)
            scaled = (part * gain_ref[:, pl.ds(first, half)]).astype(bf16)
            acc[:, :q_cols] += jnp.dot(
                scaled, wq[pl.ds(first, half), :], preferred_element_type=f32
            )
            acc[:, q_cols:] += jnp.dot(
                scaled, wkv[pl.ds(first, half), :], preferred_element_type=f32
            )
        return carry

    lax.fori_loop(0, n, project, 0)

    scale = lax.rsqrt(sumsq[...] * (1.0 / (width * n)) + 1e-05)
    cosine, sine = cos_ref[...], sin_ref[...]

    def rotary(v):
        return v * cosine + pltpu.roll(v, HEAD_SIZE // 2, 1) * sine

    for h in range(heads_here):
        d, hh = h // half_heads, h % half_heads
        v = acc[:, h * HEAD_SIZE : (h + 1) * HEAD_SIZE] * scale
        qbuf[d, 0, hh * tokens : (hh + 1) * tokens, :] = rotary(v).astype(bf16)

    def q_copy(d, s):
        return send(
            qbuf.at[d, s], qbuf.at[d, s + 1], q_send.at[d, s], q_recv.at[d, s + 1], d
        )

    def q_arrival(d, s):
        return send(qbuf.at[d, s - 1], qbuf.at[d, s], q_send.at[d, s], q_recv.at[d, s], d)

    def kv_copy(d, s):
        return send(
            kvbuf.at[d, s], kvbuf.at[d, s + 1], kv_send.at[d, s], kv_recv.at[d, s + 1], d
        )

    def kv_arrival(d, s):
        return send(kvbuf.at[d, s - 1], kvbuf.at[d, s], kv_send.at[d, s], kv_recv.at[d, s], d)

    def after(s):
        return lax.rem(s + 1, n)

    def o_copies(d, s):
        t = after(s)
        return (
            send(obuf.at[d, s], obuf.at[d, t], o_send.at[d, s], o_recv.at[d, t], d),
            send(mlbuf.at[d, s], mlbuf.at[d, t], ml_send.at[d, s], ml_recv.at[d, t], d),
        )

    def o_arrivals(d, t):
        s = lax.rem(t + n - 1, n)
        return (
            send(obuf.at[d, s], obuf.at[d, t], o_send.at[d, s], o_recv.at[d, t], d),
            send(mlbuf.at[d, s], mlbuf.at[d, t], ml_send.at[d, s], ml_recv.at[d, t], d),
        )

    for d in range(2):
        q_copy(d, 0).start()
    is_key = jnp.broadcast_to(me * kv_cols, (tokens, HEAD_SIZE)) < key_cols
    for d in range(2):
        for c in range(kv_half // HEAD_SIZE):
            a = q_cols + d * kv_half + c * HEAD_SIZE
            v = (acc[:, a : a + HEAD_SIZE] * scale).astype(bf16).astype(f32)
            turned = jnp.where(is_key, rotary(v), v)
            kvbuf[d, 0, :, c * HEAD_SIZE : (c + 1) * HEAD_SIZE] = turned.astype(bf16)
        kv_copy(d, 0).start()

    loads[2].wait()
    for g in range(KEY_VALUE_HEADS):
        a = key_cols + g * HEAD_SIZE
        vt[g * HEAD_SIZE : (g + 1) * HEAD_SIZE, :] = cache[:, a : a + HEAD_SIZE].T

    factor = HEAD_SIZE ** (-0.5) * LOG2E

    def merged(m1, l1, o1, m2, l2, o2):
        m = jnp.maximum(m1, m2)
        a, b = jnp.exp2(m1 - m), jnp.exp2(m2 - m)
        return m, l1 * a + l2 * b, o1 * a + o2 * b

    def partial(keys, values_t, q, bias):
        scores = lax.dot_general(
            keys, q, (((1,), (1,)), ((), ())), preferred_element_type=f32
        ) * factor + bias
        m = jnp.max(scores, axis=0, keepdims=True)
        p = jnp.exp2(scores - m)
        l = jnp.sum(p, axis=0, keepdims=True)
        o = jnp.dot(values_t, p.astype(bf16), preferred_element_type=f32)
        return m, l, o

    def attend(s, carry):
        for d in range(2):

            @pl.when(s > 0)
            def _():
                q_arrival(d, s).wait_recv()

            @pl.when((s > 0) & (s < n - 1))
            def _():
                q_copy(d, s).start()

        for d in range(2):

            @pl.when(s > 0)
            def _():
                kv_arrival(d, s).wait_recv()

            @pl.when((s > 0) & (s < n - 1))
            def _():
                kv_copy(d, s).start()

            owner = owner_at(d, s)
            col = pl.multiple_of(owner * kv_cols + d * kv_half, 128)
            fresh_ref[:, pl.ds(col, kv_half)] = kvbuf[d, s]

        for d in range(2):
            owner = owner_at(d, s)
            head = lax.div(owner * heads_here, group)
            first = pl.multiple_of(head * HEAD_SIZE, HEAD_SIZE)
            keys = cache[:, pl.ds(first, HEAD_SIZE)]
            values_t = vt[pl.ds(first, HEAD_SIZE), :]
            bias = bias_ref[...]
            parts = [
                partial(keys, values_t, qbuf[d, s, r : r + tokens, :], bias)
                for r in range(0, rows, tokens)
            ]

            @pl.when(s > 1)
            def _():
                for c in o_arrivals(d, s):
                    c.wait_recv()

            for i, (m, l, o) in enumerate(parts):
                span = slice(i * tokens, (i + 1) * tokens)

                @pl.when(s == 0)
                def _():
                    own_o[d, :, span] = o
                    own_ml[d, 0:1, span] = m
                    own_ml[d, 1:2, span] = l

                @pl.when(s == 1)
                def _():
                    obuf[d, s, :, span] = o.astype(bf16)
                    mlbuf[d, s, 0:1, span] = m
                    mlbuf[d, s, 1:2, span] = l
                    mlbuf[d, s, 2:8, span] = jnp.zeros((6, tokens), f32)

                @pl.when(s > 1)
                def _():
                    m3, l3, o3 = merged(
                        mlbuf[d, s, 0:1, span], mlbuf[d, s, 1:2, span],
                        obuf[d, s, :, span].astype(f32), m, l, o,
                    )
                    obuf[d, s, :, span] = o3.astype(bf16)
                    mlbuf[d, s, 0:1, span] = m3
                    mlbuf[d, s, 1:2, span] = l3

            @pl.when(s > 0)
            def _():
                for c in o_copies(d, s):
                    c.start()

        return carry

    lax.fori_loop(0, n, attend, 0)

    head = lax.div(me * heads_here, group)
    first = pl.multiple_of(head * HEAD_SIZE, HEAD_SIZE)
    fresh_keys = fresh_ref[:, pl.ds(first, HEAD_SIZE)]
    fresh_values_t = fresh_ref[
        :, pl.ds(pl.multiple_of(first + key_cols, HEAD_SIZE), HEAD_SIZE)
    ].T
    key_at = lax.broadcasted_iota(jnp.int32, (tokens, tokens), 0)
    query_at = lax.broadcasted_iota(jnp.int32, (tokens, tokens), 1)
    causal = jnp.where(key_at <= query_at, 0.0, NEG_FILL)
    for d in range(2):
        own_parts = []
        for i in range(half_heads):
            span = slice(i * tokens, (i + 1) * tokens)
            m, l, o = partial(fresh_keys, fresh_values_t, qbuf[d, 0, span, :], causal)
            own_parts.append(
                merged(own_ml[d, 0:1, span], own_ml[d, 1:2, span], own_o[d, :, span], m, l, o)
            )
        for c in o_arrivals(d, 0):
            c.wait_recv()
        for i in range(half_heads):
            span = slice(i * tokens, (i + 1) * tokens)
            _, l, o = merged(
                mlbuf[d, 0, 0:1, span], mlbuf[d, 0, 1:2, span],
                obuf[d, 0, :, span].astype(f32), *own_parts[i],
            )
            h = d * half_heads + i
            att[:, h * HEAD_SIZE : (h + 1) * HEAD_SIZE] = (o / l).T.astype(bf16)

    loads[3].wait()

    def r_copy(d, s):
        t = after(s)
        return send(rbuf.at[d, s], rbuf.at[d, t], r_send.at[d, s], r_recv.at[d, t], d)

    def r_arrival(d, t):
        s = lax.rem(t + n - 1, n)
        return send(rbuf.at[d, s], rbuf.at[d, t], r_send.at[d, s], r_recv.at[d, t], d)

    def share(d, owner):
        col = pl.multiple_of(owner * width + d * half, 128)
        return jnp.dot(att[...], wo[:, pl.ds(col, half)], preferred_element_type=f32)

    def scatter(s, carry):
        for d in range(2):
            part = share(d, owner_at(d, s))

            @pl.when(s > 1)
            def _():
                r_arrival(d, s).wait_recv()
                rbuf[d, s] = (rbuf[d, s].astype(f32) + part).astype(bf16)

            @pl.when(s == 1)
            def _():
                rbuf[d, s] = part.astype(bf16)

            r_copy(d, s).start()
        return carry

    lax.fori_loop(1, n, scatter, 0)

    def cross(d):
        return pltpu.make_async_remote_copy(
            src_ref=upd.at[d], dst_ref=landed.at[d], send_sem=x_send.at[d],
            recv_sem=x_recv.at[d], device_id={"section": sec_next},
            device_id_type=pl.DeviceIdType.MESH,
        )

    mine = [own_ref[:, d * half : (d + 1) * half].astype(f32) + share(d, me) for d in range(2)]
    for d in range(2):
        r_arrival(d, 0).wait_recv()
        upd[d] = (mine[d] + rbuf[d, 0].astype(f32)).astype(bf16)
        cross(d).start()
    for d in range(2):
        cross(d).wait_recv()
        handed_ref[:, d * half : (d + 1) * half] = landed[d]

    def sent(s, carry):
        for d in range(2):
            h_copy(d, s).wait_send()
            q_copy(d, s).wait_send()
            kv_copy(d, s).wait_send()
            for c in o_copies(d, s + 1):
                c.wait_send()
            r_copy(d, s + 1).wait_send()
        return carry

    lax.fori_loop(0, n - 1, sent, 0)
    for d in range(2):
        cross(d).wait_send()


def on_device(
    hidden, norm_gain, w_query, key_value_weight, w_out, cache_pages, prefix_len, page_owner
):
    n = lax.axis_size("tp")
    heads_here = QUERY_HEADS // n
    tokens, width = hidden.shape[1:]
    kv_cols = key_value_weight.shape[2]
    if heads_here % 2 or kv_cols % (2 * HEAD_SIZE) or n % 2 or width % 256:
        return on_device_plain(
            hidden, norm_gain, w_query, key_value_weight, w_out, cache_pages, prefix_len,
            page_owner,
        )
    sections = lax.axis_size("section")
    me = lax.axis_index("tp")
    slots = cache_pages.shape[1]
    half, half_heads = width // 2, heads_here // 2
    rows = half_heads * tokens
    cached_len = prefix_len[0, 0]
    half_head = HEAD_SIZE // 2
    inv_freq = ROPE_BASE ** (-jnp.arange(half_head, dtype=jnp.float32) * (2.0 / HEAD_SIZE))
    places = (cached_len + jnp.arange(tokens, dtype=jnp.int32)).astype(jnp.float32)
    angles = places[:, None] * inv_freq[None, :]
    cosine, sine = jnp.cos(angles), jnp.sin(angles)
    cos2 = jnp.concatenate([cosine, cosine], axis=1)
    sin2 = jnp.concatenate([-sine, sine], axis=1)
    slot_at = me * slots + jnp.arange(slots, dtype=jnp.int32)
    bias = jnp.broadcast_to(
        jnp.where(slot_at < cached_len, 0.0, NEG_FILL).astype(jnp.float32)[:, None],
        (slots, tokens),
    )
    bf16, f32 = jnp.bfloat16, jnp.float32
    q_cols = heads_here * HEAD_SIZE
    full = norm_gain.shape[1]
    kv_all = kv_cols * n
    dma = pltpu.SemaphoreType.DMA
    handed, fresh_rot = pl.pallas_call(
        functools.partial(layer_kernel, n, sections, heads_here),
        out_shape=(
            jax.ShapeDtypeStruct((tokens, width), bf16),
            jax.ShapeDtypeStruct((tokens, kv_all), bf16),
        ),
        in_specs=[VMEM] * 5 + [ANY] * 4,
        out_specs=(VMEM, VMEM),
        scratch_shapes=[
            pltpu.VMEM((full, q_cols), bf16),
            pltpu.VMEM((full, kv_cols), bf16),
            pltpu.VMEM((q_cols, full), bf16),
            pltpu.VMEM((slots, kv_all), bf16),
            pltpu.VMEM((kv_all // 2, slots), bf16),
            pltpu.VMEM((2, n, tokens, half), bf16),
            pltpu.VMEM((tokens, q_cols + kv_cols), f32),
            pltpu.VMEM((tokens, 1), f32),
            pltpu.VMEM((2, n, rows, HEAD_SIZE), bf16),
            pltpu.VMEM((2, n, HEAD_SIZE, rows), bf16),
            pltpu.VMEM((2, n, 8, rows), f32),
            pltpu.VMEM((2, HEAD_SIZE, rows), f32),
            pltpu.VMEM((2, 8, rows), f32),
            pltpu.VMEM((2, n, tokens, kv_cols // 2), bf16),
            pltpu.VMEM((tokens, q_cols), bf16),
            pltpu.VMEM((2, n, tokens, half), bf16),
            pltpu.VMEM((2, tokens, half), bf16),
            pltpu.VMEM((2, tokens, half), bf16),
            dma((4,)),
        ]
        + [dma((2, n))] * 12
        + [dma((2,))] * 2,
        compiler_params=pltpu.CompilerParams(
            collective_id=0, has_side_effects=True, vmem_limit_bytes=VMEM_BYTES
        ),
    )(
        hidden[0], norm_gain, cos2, sin2, bias, w_query[0], key_value_weight[0], w_out[0],
        cache_pages[0],
    )
    picked, _, _ = fresh_pages(fresh_rot, page_owner[0], me)
    return (handed[None], picked.reshape(1, 1, MOST, PAGE, kv_all))


def solution(mesh):
    return jax.shard_map(
        on_device,
        mesh=mesh,
        in_specs=(
            P("section", "groups", "tp"),
            P("section", None),
            P("section", None, "tp"),
            P("section", None, "tp"),
            P("section", "tp", None),
            P("section", ("groups", "tp"), None),
            P("section", "groups"),
            P("section", "groups"),
        ),
        out_specs=(P("section", "groups", "tp"), P("section", "tp", "groups", None, None)),
        check_vma=False,
    )
```

```python
import functools

import jax
import jax.numpy as jnp
import numpy as np
from jax import lax
from jax.experimental import pallas as pl
from jax.experimental.pallas import tpu as pltpu
from jax.sharding import PartitionSpec as P

QUERY_HEADS = 64
KEY_VALUE_HEADS = 8
HEAD_SIZE = 128
SPAN_TOKENS = 128
PAGE = 8
MOST = 4
NPAGE = 16


ROPE_BASE = 500000.0
NEG_FILL = -1e30


def passed_along(array, axis, by):
    length = lax.axis_size(axis)
    return lax.ppermute(array, axis, [(i, (i + by) % length) for i in range(length)])


def apply_rotary(values, token_places):
    head_width = values.shape[-1]
    half_width = head_width // 2
    inv_freq = ROPE_BASE ** (-jnp.arange(half_width, dtype=jnp.float32) * (2.0 / head_width))
    angles = token_places.astype(jnp.float32)[:, None] * inv_freq[None, :]
    cosine = jnp.cos(angles)[:, None, :]
    sine_part = jnp.sin(angles)[:, None, :]
    first_half = values[..., :half_width]
    second_half = values[..., half_width:]
    return jnp.concatenate(
        [
            first_half * cosine - second_half * sine_part,
            second_half * cosine + first_half * sine_part,
        ],
        axis=-1,
    )


def rotate_fresh(new_key_value, token_places):
    key_column_count = KEY_VALUE_HEADS * HEAD_SIZE
    rotary_output = apply_rotary(
        new_key_value[:, :key_column_count]
        .astype(jnp.float32)
        .reshape(-1, KEY_VALUE_HEADS, HEAD_SIZE),
        token_places,
    )
    return jnp.concatenate(
        [
            rotary_output.reshape(-1, key_column_count).astype(jnp.bfloat16),
            new_key_value[:, key_column_count:],
        ],
        axis=1,
    )


def fresh_pages(fresh_rot, owners, my_index):
    page_index = jnp.arange(NPAGE, dtype=jnp.int32)
    same_owner = owners[:, None] == owners[None, :]
    earlier = page_index[None, :] < page_index[:, None]
    page_rank = jnp.sum((same_owner & earlier).astype(jnp.int32), axis=1)
    slot_index = jnp.arange(MOST, dtype=jnp.int32)
    matched = (owners[None, :] == my_index) & (page_rank[None, :] == slot_index[:, None])
    flat_pages = fresh_rot.reshape(NPAGE, PAGE * fresh_rot.shape[1])
    picked = jnp.dot(
        matched.astype(jnp.bfloat16), flat_pages, preferred_element_type=jnp.float32
    ).astype(jnp.bfloat16)
    slot_page = jnp.sum(jnp.where(matched, page_index[None, :], 0), axis=1)
    slot_live = jnp.any(matched, axis=1)
    return (picked, slot_page, slot_live)


def on_device_plain(
    hidden, norm_gain, w_query, key_value_weight, w_out, cache_pages, prefix_len, page_owner
):
    tp_size = lax.axis_size("tp")
    my_index = lax.axis_index("tp")
    heads_here = QUERY_HEADS // tp_size
    query_group_width = QUERY_HEADS // KEY_VALUE_HEADS
    key_column_count = KEY_VALUE_HEADS * HEAD_SIZE
    own_rows = hidden[0]
    full_rows = lax.all_gather(own_rows, "tp", axis=1, tiled=True)
    rows_f32 = full_rows.astype(jnp.float32)
    normed = (
        rows_f32
        * lax.rsqrt(jnp.mean(rows_f32 * rows_f32, axis=1, keepdims=True) + 1e-05)
        * norm_gain[0][None, :]
    ).astype(jnp.bfloat16)
    cached_len = prefix_len[0, 0]
    token_index = jnp.arange(SPAN_TOKENS, dtype=jnp.int32)
    token_places = cached_len + token_index
    query_f32 = jnp.dot(normed, w_query[0], preferred_element_type=jnp.float32).reshape(
        SPAN_TOKENS, heads_here, HEAD_SIZE
    )
    queries = (
        apply_rotary(query_f32, token_places)
        .astype(jnp.bfloat16)
        .reshape(SPAN_TOKENS, heads_here * HEAD_SIZE)
    )
    fresh_part = jnp.dot(normed, key_value_weight[0], preferred_element_type=jnp.float32).astype(
        jnp.bfloat16
    )
    cached = cache_pages[0]
    slots_here = cached.shape[0]
    head_table = np.arange(tp_size) * heads_here // query_group_width
    by_head = jnp.transpose(
        cached.reshape(slots_here, 2, KEY_VALUE_HEADS, HEAD_SIZE), (2, 0, 1, 3)
    ).reshape(KEY_VALUE_HEADS, slots_here, 2 * HEAD_SIZE)
    outgoing = jnp.stack([by_head[int(h)] for h in head_table])
    arrived = lax.all_to_all(outgoing, "tp", split_axis=0, concat_axis=0, tiled=True)
    fresh_all = lax.all_gather(fresh_part, "tp", axis=1, tiled=True)
    fresh_rot = rotate_fresh(fresh_all, token_places)
    picked, slot_page, slot_live = fresh_pages(fresh_rot, page_owner[0], my_index)
    kv_head = my_index * heads_here // query_group_width
    local_key_rows = lax.dynamic_slice_in_dim(fresh_rot, kv_head * HEAD_SIZE, HEAD_SIZE, 1)
    local_value_rows = lax.dynamic_slice_in_dim(
        fresh_rot, key_column_count + kv_head * HEAD_SIZE, HEAD_SIZE, 1
    )
    all_keys = jnp.concatenate(
        [arrived[:, :, :HEAD_SIZE].reshape(tp_size * slots_here, HEAD_SIZE), local_key_rows], axis=0
    )
    all_values = jnp.concatenate(
        [arrived[:, :, HEAD_SIZE:].reshape(tp_size * slots_here, HEAD_SIZE), local_value_rows],
        axis=0,
    )
    cache_mask = jnp.broadcast_to(
        (jnp.arange(tp_size * slots_here, dtype=jnp.int32) < cached_len)[None, :],
        (SPAN_TOKENS, tp_size * slots_here),
    )
    fresh_mask = token_index[None, :] <= token_index[:, None]
    visible_key_mask = jnp.concatenate([cache_mask, fresh_mask], axis=1)
    head_queries = queries.reshape(SPAN_TOKENS, heads_here, HEAD_SIZE)

    def per_query(head_slot):
        one_head = lax.dynamic_index_in_dim(head_queries, head_slot, 1, keepdims=False)
        scores = jnp.einsum(
            "td,kd->tk", one_head, all_keys, preferred_element_type=jnp.float32
        ) * HEAD_SIZE ** (-0.5)
        scores = jnp.where(visible_key_mask, scores, NEG_FILL)
        top_score = jnp.max(scores, axis=1, keepdims=True)
        weights = jnp.exp(scores - top_score)
        denominator = jnp.sum(weights, axis=1, keepdims=True)
        summed = jnp.dot(
            weights.astype(jnp.bfloat16), all_values, preferred_element_type=jnp.float32
        )
        return summed / denominator

    outputs = lax.map(per_query, jnp.arange(heads_here, dtype=jnp.int32))
    attended = (
        jnp.transpose(outputs, (1, 0, 2))
        .reshape(SPAN_TOKENS, heads_here * HEAD_SIZE)
        .astype(jnp.bfloat16)
    )
    out_weight = w_out[0]
    block_share = lax.psum_scatter(
        lax.dot_general(
            out_weight, attended, (((0,), (1,)), ((), ())), preferred_element_type=jnp.float32
        ).astype(jnp.bfloat16),
        "tp",
        scatter_dimension=0,
        tiled=True,
    ).astype(jnp.float32)
    updated = (own_rows.astype(jnp.float32) + block_share.T).astype(jnp.bfloat16)
    handed = passed_along(updated, "section", 1)
    return (handed[None], picked.reshape(1, 1, MOST, PAGE, 2 * key_column_count))


LOG2E = 1.4426950408889634
VMEM_BYTES = 60 * 1024 * 1024
ANY = pl.BlockSpec(memory_space=pl.ANY)
VMEM = pl.BlockSpec(memory_space=pltpu.VMEM)


def layer_kernel(
    n, sections, heads_here,
    own_ref, gain_ref, cos_ref, sin_ref, bias_ref, wq_hbm, wkv_hbm, wo_hbm, cache_hbm,
    handed_ref, fresh_ref,
    wq, wkv, wo, cache, vt, hbuf, acc, sumsq, qbuf, obuf, mlbuf, own_o, own_ml, kvbuf, att,
    rbuf, upd, landed,
    w_sem, q_send, q_recv, kv_send, kv_recv, o_send, o_recv, ml_send, ml_recv,
    h_send, h_recv, r_send, r_recv, x_send, x_recv,
):
    f32, bf16 = jnp.float32, jnp.bfloat16
    tokens, width = own_ref.shape
    half = width // 2
    half_heads = heads_here // 2
    q_cols = heads_here * HEAD_SIZE
    kv_cols = wkv.shape[1]
    kv_half = kv_cols // 2
    key_cols = KEY_VALUE_HEADS * HEAD_SIZE
    rows = half_heads * tokens
    group = QUERY_HEADS // KEY_VALUE_HEADS

    me = lax.axis_index("tp")
    z, y = lax.div(me, 2), lax.rem(me, 2)
    place = y * (n - 1 - z) + (1 - y) * z

    def at_place(p):
        p = lax.rem(p + 2 * n, n)
        c = lax.div(p, n // 2)
        return (1 - c) * (2 * p) + c * (2 * (n - 1 - p) + 1)

    to = (at_place(place + 1), at_place(place - 1))

    def owner_at(d, s):
        return at_place(place - s) if d == 0 else at_place(place + s)

    def send(src, dst, ssem, rsem, d):
        return pltpu.make_async_remote_copy(
            src_ref=src, dst_ref=dst, send_sem=ssem, recv_sem=rsem,
            device_id={"tp": to[d]}, device_id_type=pl.DeviceIdType.MESH,
        )

    loads = [
        pltpu.make_async_copy(src, dst, w_sem.at[i])
        for i, (src, dst) in enumerate(
            ((wq_hbm, wq), (wkv_hbm, wkv), (cache_hbm, cache), (wo_hbm, wo))
        )
    ]
    loads[0].start()
    loads[1].start()

    sec = lax.axis_index("section")
    sec_next = lax.rem(sec + 1, sections)
    sec_prev = lax.rem(sec + sections - 1, sections)
    barrier = pltpu.get_barrier_semaphore()
    for d in range(2):
        pl.semaphore_signal(
            barrier, inc=1, device_id={"tp": to[d]}, device_id_type=pl.DeviceIdType.MESH
        )
    pl.semaphore_signal(
        barrier, inc=1, device_id={"section": sec_prev}, device_id_type=pl.DeviceIdType.MESH
    )
    for d in range(2):
        hbuf[d, 0] = own_ref[:, d * half : (d + 1) * half]
    acc[...] = jnp.zeros_like(acc)
    sumsq[...] = jnp.zeros_like(sumsq)
    pl.semaphore_wait(barrier, 3)

    piece = tokens // 2

    def h_copy(d, s, c):
        span = pl.ds(c * piece, piece)
        return send(
            hbuf.at[d, s, span], hbuf.at[d, s + 1, span],
            h_send.at[d, s, c], h_recv.at[d, s + 1, c], d,
        )

    def h_arrival(d, s, c):
        span = pl.ds(c * piece, piece)
        return send(
            hbuf.at[d, s - 1, span], hbuf.at[d, s, span],
            h_send.at[d, s, c], h_recv.at[d, s, c], d,
        )

    turns = n // 2
    turn_heads = KEY_VALUE_HEADS // turns

    def project(s, carry):
        for c in range(2):
            for d in range(2):

                @pl.when(s > 0)
                def _():
                    h_arrival(d, s, c).wait_recv()

                @pl.when(s < n - 1)
                def _():
                    h_copy(d, s, c).start()

        @pl.when(s == n - turns)
        def _():
            loads[2].wait()

        @pl.when(s >= n - turns)
        def _():
            for k in range(turn_heads):
                g = (s - (n - turns)) * turn_heads + k
                a = pl.multiple_of(g * HEAD_SIZE, HEAD_SIZE)
                b = pl.multiple_of(g * HEAD_SIZE + key_cols, HEAD_SIZE)
                vt[pl.ds(a, HEAD_SIZE), :] = cache[:, pl.ds(b, HEAD_SIZE)].T

        @pl.when(s == 0)
        def _():
            loads[0].wait()
            loads[1].wait()
            loads[2].start()
            loads[3].start()

        for d in range(2):
            first = pl.multiple_of(owner_at(d, s) * width + d * half, 128)
            part = hbuf[d, s].astype(f32)
            sumsq[...] += jnp.sum(part * part, axis=1, keepdims=True)
            scaled = (part * gain_ref[:, pl.ds(first, half)]).astype(bf16)
            acc[:, :q_cols] += jnp.dot(
                scaled, wq[pl.ds(first, half), :], preferred_element_type=f32
            )
            acc[:, q_cols:] += jnp.dot(
                scaled, wkv[pl.ds(first, half), :], preferred_element_type=f32
            )
        return carry

    lax.fori_loop(0, n, project, 0)

    scale = lax.rsqrt(sumsq[...] * (1.0 / (width * n)) + 1e-05)
    cosine, sine = cos_ref[...], sin_ref[...]

    def rotary(v):
        return v * cosine + pltpu.roll(v, HEAD_SIZE // 2, 1) * sine

    for h in range(heads_here):
        d, hh = h // half_heads, h % half_heads
        v = acc[:, h * HEAD_SIZE : (h + 1) * HEAD_SIZE] * scale
        qbuf[d, 0, hh * tokens : (hh + 1) * tokens, :] = rotary(v).astype(bf16)

    def q_copy(d, s):
        return send(
            qbuf.at[d, s], qbuf.at[d, s + 1], q_send.at[d, s], q_recv.at[d, s + 1], d
        )

    def q_arrival(d, s):
        return send(qbuf.at[d, s - 1], qbuf.at[d, s], q_send.at[d, s], q_recv.at[d, s], d)

    def kv_copy(d, s):
        return send(
            kvbuf.at[d, s], kvbuf.at[d, s + 1], kv_send.at[d, s], kv_recv.at[d, s + 1], d
        )

    def kv_arrival(d, s):
        return send(kvbuf.at[d, s - 1], kvbuf.at[d, s], kv_send.at[d, s], kv_recv.at[d, s], d)

    def after(s):
        return lax.rem(s + 1, n)

    def o_copies(d, s):
        t = after(s)
        return (
            send(obuf.at[d, s], obuf.at[d, t], o_send.at[d, s], o_recv.at[d, t], d),
            send(mlbuf.at[d, s], mlbuf.at[d, t], ml_send.at[d, s], ml_recv.at[d, t], d),
        )

    def o_arrivals(d, t):
        s = lax.rem(t + n - 1, n)
        return (
            send(obuf.at[d, s], obuf.at[d, t], o_send.at[d, s], o_recv.at[d, t], d),
            send(mlbuf.at[d, s], mlbuf.at[d, t], ml_send.at[d, s], ml_recv.at[d, t], d),
        )

    for d in range(2):
        q_copy(d, 0).start()
    is_key = jnp.broadcast_to(me * kv_cols, (tokens, HEAD_SIZE)) < key_cols
    for d in range(2):
        for c in range(kv_half // HEAD_SIZE):
            a = q_cols + d * kv_half + c * HEAD_SIZE
            v = (acc[:, a : a + HEAD_SIZE] * scale).astype(bf16).astype(f32)
            turned = jnp.where(is_key, rotary(v), v)
            kvbuf[d, 0, :, c * HEAD_SIZE : (c + 1) * HEAD_SIZE] = turned.astype(bf16)
        kv_copy(d, 0).start()

    factor = HEAD_SIZE ** (-0.5) * LOG2E

    def merged(m1, l1, o1, m2, l2, o2):
        m = jnp.maximum(m1, m2)
        a, b = jnp.exp2(m1 - m), jnp.exp2(m2 - m)
        return m, l1 * a + l2 * b, o1 * a + o2 * b

    def partial(keys, values_t, q, bias):
        scores = lax.dot_general(
            keys, q, (((1,), (1,)), ((), ())), preferred_element_type=f32
        ) * factor + bias
        m = jnp.max(scores, axis=0, keepdims=True)
        p = jnp.exp2(scores - m)
        l = jnp.sum(p, axis=0, keepdims=True)
        o = jnp.dot(values_t, p.astype(bf16), preferred_element_type=f32)
        return m, l, o

    def attend(s, carry):
        for d in range(2):

            @pl.when(s > 0)
            def _():
                q_arrival(d, s).wait_recv()

            @pl.when((s > 0) & (s < n - 1))
            def _():
                q_copy(d, s).start()

        for d in range(2):

            @pl.when(s > 0)
            def _():
                kv_arrival(d, s).wait_recv()

            @pl.when((s > 0) & (s < n - 1))
            def _():
                kv_copy(d, s).start()

            owner = owner_at(d, s)
            col = pl.multiple_of(owner * kv_cols + d * kv_half, 128)
            fresh_ref[:, pl.ds(col, kv_half)] = kvbuf[d, s]

        for d in range(2):
            owner = owner_at(d, s)
            head = lax.div(owner * heads_here, group)
            first = pl.multiple_of(head * HEAD_SIZE, HEAD_SIZE)
            keys = cache[:, pl.ds(first, HEAD_SIZE)]
            values_t = vt[pl.ds(first, HEAD_SIZE), :]
            bias = bias_ref[...]
            parts = [
                partial(keys, values_t, qbuf[d, s, r : r + tokens, :], bias)
                for r in range(0, rows, tokens)
            ]

            @pl.when(s > 1)
            def _():
                for c in o_arrivals(d, s):
                    c.wait_recv()

            for i, (m, l, o) in enumerate(parts):
                span = slice(i * tokens, (i + 1) * tokens)

                @pl.when(s == 0)
                def _():
                    own_o[d, :, span] = o
                    own_ml[d, 0:1, span] = m
                    own_ml[d, 1:2, span] = l

                @pl.when(s == 1)
                def _():
                    obuf[d, s, :, span] = o.astype(bf16)
                    mlbuf[d, s, 0:1, span] = m
                    mlbuf[d, s, 1:2, span] = l

                @pl.when(s > 1)
                def _():
                    m3, l3, o3 = merged(
                        mlbuf[d, s, 0:1, span], mlbuf[d, s, 1:2, span],
                        obuf[d, s, :, span].astype(f32), m, l, o,
                    )
                    obuf[d, s, :, span] = o3.astype(bf16)
                    mlbuf[d, s, 0:1, span] = m3
                    mlbuf[d, s, 1:2, span] = l3

            @pl.when(s > 0)
            def _():
                for c in o_copies(d, s):
                    c.start()

        return carry

    lax.fori_loop(0, n, attend, 0)

    head = lax.div(me * heads_here, group)
    first = pl.multiple_of(head * HEAD_SIZE, HEAD_SIZE)
    fresh_keys = fresh_ref[:, pl.ds(first, HEAD_SIZE)]
    fresh_values_t = fresh_ref[
        :, pl.ds(pl.multiple_of(first + key_cols, HEAD_SIZE), HEAD_SIZE)
    ].T
    key_at = lax.broadcasted_iota(jnp.int32, (tokens, tokens), 0)
    query_at = lax.broadcasted_iota(jnp.int32, (tokens, tokens), 1)
    causal = jnp.where(key_at <= query_at, 0.0, NEG_FILL)
    for d in range(2):
        own_parts = []
        for i in range(half_heads):
            span = slice(i * tokens, (i + 1) * tokens)
            m, l, o = partial(fresh_keys, fresh_values_t, qbuf[d, 0, span, :], causal)
            own_parts.append(
                merged(own_ml[d, 0:1, span], own_ml[d, 1:2, span], own_o[d, :, span], m, l, o)
            )
        for c in o_arrivals(d, 0):
            c.wait_recv()
        for i in range(half_heads):
            span = slice(i * tokens, (i + 1) * tokens)
            _, l, o = merged(
                mlbuf[d, 0, 0:1, span], mlbuf[d, 0, 1:2, span],
                obuf[d, 0, :, span].astype(f32), *own_parts[i],
            )
            h = d * half_heads + i
            att[:, h * HEAD_SIZE : (h + 1) * HEAD_SIZE] = (o / l).T.astype(bf16)

    loads[3].wait()

    def r_between(d, s, t, c):
        span = pl.ds(c * piece, piece)
        return send(
            rbuf.at[d, s, span], rbuf.at[d, t, span], r_send.at[d, s, c], r_recv.at[d, t, c], d
        )

    def r_copy(d, s, c):
        return r_between(d, s, after(s), c)

    def r_arrival(d, t, c):
        return r_between(d, lax.rem(t + n - 1, n), t, c)

    def share(d, owner):
        col = pl.multiple_of(owner * width + d * half, 128)
        return jnp.dot(att[...], wo[:, pl.ds(col, half)], preferred_element_type=f32)

    def scatter(s, carry):
        parts = [share(d, owner_at(d, s)) for d in range(2)]
        for c in range(2):
            span = slice(c * piece, (c + 1) * piece)
            for d in range(2):

                @pl.when(s > 1)
                def _():
                    r_arrival(d, s, c).wait_recv()
                    rbuf[d, s, span] = (rbuf[d, s, span].astype(f32) + parts[d][span]).astype(bf16)

                @pl.when(s == 1)
                def _():
                    rbuf[d, s, span] = parts[d][span].astype(bf16)

                r_copy(d, s, c).start()
        return carry

    lax.fori_loop(1, n, scatter, 0)

    def cross(d):
        return pltpu.make_async_remote_copy(
            src_ref=upd.at[d], dst_ref=landed.at[d], send_sem=x_send.at[d],
            recv_sem=x_recv.at[d], device_id={"section": sec_next},
            device_id_type=pl.DeviceIdType.MESH,
        )

    mine = [own_ref[:, d * half : (d + 1) * half].astype(f32) + share(d, me) for d in range(2)]
    for d in range(2):
        for c in range(2):
            r_arrival(d, 0, c).wait_recv()
        upd[d] = (mine[d] + rbuf[d, 0].astype(f32)).astype(bf16)
        cross(d).start()
    for d in range(2):
        cross(d).wait_recv()
        handed_ref[:, d * half : (d + 1) * half] = landed[d]

    def sent(s, carry):
        for d in range(2):
            for c in range(2):
                h_copy(d, s, c).wait_send()
                r_copy(d, s + 1, c).wait_send()
            q_copy(d, s).wait_send()
            kv_copy(d, s).wait_send()
            for c in o_copies(d, s + 1):
                c.wait_send()
        return carry

    lax.fori_loop(0, n - 1, sent, 0)
    for d in range(2):
        cross(d).wait_send()


def on_device(
    hidden, norm_gain, w_query, key_value_weight, w_out, cache_pages, prefix_len, page_owner
):
    n = lax.axis_size("tp")
    heads_here = QUERY_HEADS // n
    tokens, width = hidden.shape[1:]
    kv_cols = key_value_weight.shape[2]
    if heads_here % 2 or kv_cols % (2 * HEAD_SIZE) or KEY_VALUE_HEADS % (n // 2) or n % 2 or tokens % 32 or width % 256:
        return on_device_plain(
            hidden, norm_gain, w_query, key_value_weight, w_out, cache_pages, prefix_len,
            page_owner,
        )
    sections = lax.axis_size("section")
    me = lax.axis_index("tp")
    slots = cache_pages.shape[1]
    half, half_heads = width // 2, heads_here // 2
    rows = half_heads * tokens
    cached_len = prefix_len[0, 0]
    half_head = HEAD_SIZE // 2
    inv_freq = ROPE_BASE ** (-jnp.arange(half_head, dtype=jnp.float32) * (2.0 / HEAD_SIZE))
    places = (cached_len + jnp.arange(tokens, dtype=jnp.int32)).astype(jnp.float32)
    angles = places[:, None] * inv_freq[None, :]
    cosine, sine = jnp.cos(angles), jnp.sin(angles)
    cos2 = jnp.concatenate([cosine, cosine], axis=1)
    sin2 = jnp.concatenate([-sine, sine], axis=1)
    slot_at = me * slots + jnp.arange(slots, dtype=jnp.int32)
    bias = jnp.broadcast_to(
        jnp.where(slot_at < cached_len, 0.0, NEG_FILL).astype(jnp.float32)[:, None],
        (slots, tokens),
    )
    bf16, f32 = jnp.bfloat16, jnp.float32
    q_cols = heads_here * HEAD_SIZE
    full = norm_gain.shape[1]
    kv_all = kv_cols * n
    dma = pltpu.SemaphoreType.DMA
    handed, fresh_rot = pl.pallas_call(
        functools.partial(layer_kernel, n, sections, heads_here),
        out_shape=(
            jax.ShapeDtypeStruct((tokens, width), bf16),
            jax.ShapeDtypeStruct((tokens, kv_all), bf16),
        ),
        in_specs=[VMEM] * 5 + [ANY] * 4,
        out_specs=(VMEM, VMEM),
        scratch_shapes=[
            pltpu.VMEM((full, q_cols), bf16),
            pltpu.VMEM((full, kv_cols), bf16),
            pltpu.VMEM((q_cols, full), bf16),
            pltpu.VMEM((slots, kv_all), bf16),
            pltpu.VMEM((kv_all // 2, slots), bf16),
            pltpu.VMEM((2, n, tokens, half), bf16),
            pltpu.VMEM((tokens, q_cols + kv_cols), f32),
            pltpu.VMEM((tokens, 1), f32),
            pltpu.VMEM((2, n, rows, HEAD_SIZE), bf16),
            pltpu.VMEM((2, n, HEAD_SIZE, rows), bf16),
            pltpu.VMEM((2, n, 2, rows), f32),
            pltpu.VMEM((2, HEAD_SIZE, rows), f32),
            pltpu.VMEM((2, 8, rows), f32),
            pltpu.VMEM((2, n, tokens, kv_cols // 2), bf16),
            pltpu.VMEM((tokens, q_cols), bf16),
            pltpu.VMEM((2, n, tokens, half), bf16),
            pltpu.VMEM((2, tokens, half), bf16),
            pltpu.VMEM((2, tokens, half), bf16),
            dma((4,)),
        ]
        + [dma((2, n))] * 8
        + [dma((2, n, 2))] * 4
        + [dma((2,))] * 2,
        compiler_params=pltpu.CompilerParams(
            collective_id=0, has_side_effects=True, vmem_limit_bytes=VMEM_BYTES
        ),
    )(
        hidden[0], norm_gain, cos2, sin2, bias, w_query[0], key_value_weight[0], w_out[0],
        cache_pages[0],
    )
    picked, _, _ = fresh_pages(fresh_rot, page_owner[0], me)
    return (handed[None], picked.reshape(1, 1, MOST, PAGE, kv_all))


def solution(mesh):
    return jax.shard_map(
        on_device,
        mesh=mesh,
        in_specs=(
            P("section", "groups", "tp"),
            P("section", None),
            P("section", None, "tp"),
            P("section", None, "tp"),
            P("section", "tp", None),
            P("section", ("groups", "tp"), None),
            P("section", "groups"),
            P("section", "groups"),
        ),
        out_specs=(P("section", "groups", "tp"), P("section", "tp", "groups", None, None)),
        check_vma=False,
    )
```

```python
import functools

import jax
import jax.numpy as jnp
import numpy as np
from jax import lax
from jax.experimental import pallas as pl
from jax.experimental.pallas import tpu as pltpu
from jax.sharding import PartitionSpec as P

QUERY_HEADS = 64
KEY_VALUE_HEADS = 8
HEAD_SIZE = 128
SPAN_TOKENS = 128
PAGE = 8
MOST = 4
NPAGE = 16


ROPE_BASE = 500000.0
NEG_FILL = -1e30


def passed_along(array, axis, by):
    length = lax.axis_size(axis)
    return lax.ppermute(array, axis, [(i, (i + by) % length) for i in range(length)])


def apply_rotary(values, token_places):
    head_width = values.shape[-1]
    half_width = head_width // 2
    inv_freq = ROPE_BASE ** (-jnp.arange(half_width, dtype=jnp.float32) * (2.0 / head_width))
    angles = token_places.astype(jnp.float32)[:, None] * inv_freq[None, :]
    cosine = jnp.cos(angles)[:, None, :]
    sine_part = jnp.sin(angles)[:, None, :]
    first_half = values[..., :half_width]
    second_half = values[..., half_width:]
    return jnp.concatenate(
        [
            first_half * cosine - second_half * sine_part,
            second_half * cosine + first_half * sine_part,
        ],
        axis=-1,
    )


def rotate_fresh(new_key_value, token_places):
    key_column_count = KEY_VALUE_HEADS * HEAD_SIZE
    rotary_output = apply_rotary(
        new_key_value[:, :key_column_count]
        .astype(jnp.float32)
        .reshape(-1, KEY_VALUE_HEADS, HEAD_SIZE),
        token_places,
    )
    return jnp.concatenate(
        [
            rotary_output.reshape(-1, key_column_count).astype(jnp.bfloat16),
            new_key_value[:, key_column_count:],
        ],
        axis=1,
    )


def fresh_pages(fresh_rot, owners, my_index):
    page_index = jnp.arange(NPAGE, dtype=jnp.int32)
    same_owner = owners[:, None] == owners[None, :]
    earlier = page_index[None, :] < page_index[:, None]
    page_rank = jnp.sum((same_owner & earlier).astype(jnp.int32), axis=1)
    slot_index = jnp.arange(MOST, dtype=jnp.int32)
    matched = (owners[None, :] == my_index) & (page_rank[None, :] == slot_index[:, None])
    flat_pages = fresh_rot.reshape(NPAGE, PAGE * fresh_rot.shape[1])
    picked = jnp.dot(
        matched.astype(jnp.bfloat16), flat_pages, preferred_element_type=jnp.float32
    ).astype(jnp.bfloat16)
    slot_page = jnp.sum(jnp.where(matched, page_index[None, :], 0), axis=1)
    slot_live = jnp.any(matched, axis=1)
    return (picked, slot_page, slot_live)


def on_device_plain(
    hidden, norm_gain, w_query, key_value_weight, w_out, cache_pages, prefix_len, page_owner
):
    tp_size = lax.axis_size("tp")
    my_index = lax.axis_index("tp")
    heads_here = QUERY_HEADS // tp_size
    query_group_width = QUERY_HEADS // KEY_VALUE_HEADS
    key_column_count = KEY_VALUE_HEADS * HEAD_SIZE
    own_rows = hidden[0]
    full_rows = lax.all_gather(own_rows, "tp", axis=1, tiled=True)
    rows_f32 = full_rows.astype(jnp.float32)
    normed = (
        rows_f32
        * lax.rsqrt(jnp.mean(rows_f32 * rows_f32, axis=1, keepdims=True) + 1e-05)
        * norm_gain[0][None, :]
    ).astype(jnp.bfloat16)
    cached_len = prefix_len[0, 0]
    token_index = jnp.arange(SPAN_TOKENS, dtype=jnp.int32)
    token_places = cached_len + token_index
    query_f32 = jnp.dot(normed, w_query[0], preferred_element_type=jnp.float32).reshape(
        SPAN_TOKENS, heads_here, HEAD_SIZE
    )
    queries = (
        apply_rotary(query_f32, token_places)
        .astype(jnp.bfloat16)
        .reshape(SPAN_TOKENS, heads_here * HEAD_SIZE)
    )
    fresh_part = jnp.dot(normed, key_value_weight[0], preferred_element_type=jnp.float32).astype(
        jnp.bfloat16
    )
    cached = cache_pages[0]
    slots_here = cached.shape[0]
    head_table = np.arange(tp_size) * heads_here // query_group_width
    by_head = jnp.transpose(
        cached.reshape(slots_here, 2, KEY_VALUE_HEADS, HEAD_SIZE), (2, 0, 1, 3)
    ).reshape(KEY_VALUE_HEADS, slots_here, 2 * HEAD_SIZE)
    outgoing = jnp.stack([by_head[int(h)] for h in head_table])
    arrived = lax.all_to_all(outgoing, "tp", split_axis=0, concat_axis=0, tiled=True)
    fresh_all = lax.all_gather(fresh_part, "tp", axis=1, tiled=True)
    fresh_rot = rotate_fresh(fresh_all, token_places)
    picked, slot_page, slot_live = fresh_pages(fresh_rot, page_owner[0], my_index)
    kv_head = my_index * heads_here // query_group_width
    local_key_rows = lax.dynamic_slice_in_dim(fresh_rot, kv_head * HEAD_SIZE, HEAD_SIZE, 1)
    local_value_rows = lax.dynamic_slice_in_dim(
        fresh_rot, key_column_count + kv_head * HEAD_SIZE, HEAD_SIZE, 1
    )
    all_keys = jnp.concatenate(
        [arrived[:, :, :HEAD_SIZE].reshape(tp_size * slots_here, HEAD_SIZE), local_key_rows], axis=0
    )
    all_values = jnp.concatenate(
        [arrived[:, :, HEAD_SIZE:].reshape(tp_size * slots_here, HEAD_SIZE), local_value_rows],
        axis=0,
    )
    cache_mask = jnp.broadcast_to(
        (jnp.arange(tp_size * slots_here, dtype=jnp.int32) < cached_len)[None, :],
        (SPAN_TOKENS, tp_size * slots_here),
    )
    fresh_mask = token_index[None, :] <= token_index[:, None]
    visible_key_mask = jnp.concatenate([cache_mask, fresh_mask], axis=1)
    head_queries = queries.reshape(SPAN_TOKENS, heads_here, HEAD_SIZE)

    def per_query(head_slot):
        one_head = lax.dynamic_index_in_dim(head_queries, head_slot, 1, keepdims=False)
        scores = jnp.einsum(
            "td,kd->tk", one_head, all_keys, preferred_element_type=jnp.float32
        ) * HEAD_SIZE ** (-0.5)
        scores = jnp.where(visible_key_mask, scores, NEG_FILL)
        top_score = jnp.max(scores, axis=1, keepdims=True)
        weights = jnp.exp(scores - top_score)
        denominator = jnp.sum(weights, axis=1, keepdims=True)
        summed = jnp.dot(
            weights.astype(jnp.bfloat16), all_values, preferred_element_type=jnp.float32
        )
        return summed / denominator

    outputs = lax.map(per_query, jnp.arange(heads_here, dtype=jnp.int32))
    attended = (
        jnp.transpose(outputs, (1, 0, 2))
        .reshape(SPAN_TOKENS, heads_here * HEAD_SIZE)
        .astype(jnp.bfloat16)
    )
    out_weight = w_out[0]
    block_share = lax.psum_scatter(
        lax.dot_general(
            out_weight, attended, (((0,), (1,)), ((), ())), preferred_element_type=jnp.float32
        ).astype(jnp.bfloat16),
        "tp",
        scatter_dimension=0,
        tiled=True,
    ).astype(jnp.float32)
    updated = (own_rows.astype(jnp.float32) + block_share.T).astype(jnp.bfloat16)
    handed = passed_along(updated, "section", 1)
    return (handed[None], picked.reshape(1, 1, MOST, PAGE, 2 * key_column_count))


LOG2E = 1.4426950408889634
VMEM_BYTES = 60 * 1024 * 1024
ANY = pl.BlockSpec(memory_space=pl.ANY)
VMEM = pl.BlockSpec(memory_space=pltpu.VMEM)


def layer_kernel(
    n, sections, heads_here,
    own_ref, gain_ref, cos_ref, sin_ref, bias_ref, wq_hbm, wkv_hbm, wo_hbm, cache_hbm,
    handed_ref, fresh_ref,
    wq, wkv, wo, cache, vt, hbuf, acc, sumsq, qbuf, obuf, mlbuf, own_o, own_ml, kvbuf, att,
    rbuf, upd, landed,
    w_sem, q_send, q_recv, kv_send, kv_recv,
    o_send, o_recv, ml_send, ml_recv, h_send, h_recv, r_send, r_recv, x_send, x_recv,
):
    f32, bf16 = jnp.float32, jnp.bfloat16
    tokens, width = own_ref.shape
    half = width // 2
    half_heads = heads_here // 2
    q_cols = heads_here * HEAD_SIZE
    kv_cols = wkv.shape[1]
    kv_half = kv_cols // 2
    key_cols = KEY_VALUE_HEADS * HEAD_SIZE
    rows = half_heads * tokens
    group = QUERY_HEADS // KEY_VALUE_HEADS

    me = lax.axis_index("tp")
    z, y = lax.div(me, 2), lax.rem(me, 2)
    place = y * (n - 1 - z) + (1 - y) * z

    def at_place(p):
        p = lax.rem(p + 2 * n, n)
        c = lax.div(p, n // 2)
        return (1 - c) * (2 * p) + c * (2 * (n - 1 - p) + 1)

    to = (at_place(place + 1), at_place(place - 1))

    def owner_at(d, s):
        return at_place(place - s) if d == 0 else at_place(place + s)

    def send(src, dst, ssem, rsem, d):
        return pltpu.make_async_remote_copy(
            src_ref=src, dst_ref=dst, send_sem=ssem, recv_sem=rsem,
            device_id={"tp": to[d]}, device_id_type=pl.DeviceIdType.MESH,
        )

    loads = [
        pltpu.make_async_copy(src, dst, w_sem.at[i])
        for i, (src, dst) in enumerate(
            ((wq_hbm, wq), (wkv_hbm, wkv), (cache_hbm, cache), (wo_hbm, wo))
        )
    ]
    loads[0].start()
    loads[1].start()

    sec = lax.axis_index("section")
    sec_next = lax.rem(sec + 1, sections)
    sec_prev = lax.rem(sec + sections - 1, sections)
    barrier = pltpu.get_barrier_semaphore()
    for d in range(2):
        pl.semaphore_signal(
            barrier, inc=1, device_id={"tp": to[d]}, device_id_type=pl.DeviceIdType.MESH
        )
    pl.semaphore_signal(
        barrier, inc=1, device_id={"section": sec_prev}, device_id_type=pl.DeviceIdType.MESH
    )
    for d in range(2):
        hbuf[d, 0] = own_ref[:, d * half : (d + 1) * half]
    acc[...] = jnp.zeros_like(acc)
    sumsq[...] = jnp.zeros_like(sumsq)
    pl.semaphore_wait(barrier, 3)

    piece = tokens // 2

    def h_copy(d, s, c):
        span = pl.ds(c * piece, piece)
        return send(
            hbuf.at[d, s, span], hbuf.at[d, s + 1, span],
            h_send.at[d, s, c], h_recv.at[d, s + 1, c], d,
        )

    def h_arrival(d, s, c):
        span = pl.ds(c * piece, piece)
        return send(
            hbuf.at[d, s - 1, span], hbuf.at[d, s, span],
            h_send.at[d, s, c], h_recv.at[d, s, c], d,
        )

    turns = n // 2
    turn_heads = KEY_VALUE_HEADS // turns

    def project(s, carry):
        for c in range(2):
            for d in range(2):

                @pl.when(s > 0)
                def _():
                    h_arrival(d, s, c).wait_recv()

                @pl.when(s < n - 1)
                def _():
                    h_copy(d, s, c).start()

        @pl.when(s == n - turns)
        def _():
            loads[2].wait()

        @pl.when(s >= n - turns)
        def _():
            for k in range(turn_heads):
                g = (s - (n - turns)) * turn_heads + k
                a = pl.multiple_of(g * HEAD_SIZE, HEAD_SIZE)
                b = pl.multiple_of(g * HEAD_SIZE + key_cols, HEAD_SIZE)
                vt[pl.ds(a, HEAD_SIZE), :] = cache[:, pl.ds(b, HEAD_SIZE)].T

        @pl.when(s == 0)
        def _():
            loads[0].wait()
            loads[1].wait()
            loads[2].start()
            loads[3].start()

        for d in range(2):
            first = pl.multiple_of(owner_at(d, s) * width + d * half, 128)
            part = hbuf[d, s].astype(f32)
            sumsq[...] += jnp.sum(part * part, axis=1, keepdims=True)
            scaled = (part * gain_ref[:, pl.ds(first, half)]).astype(bf16)
            acc[:, :q_cols] += jnp.dot(
                scaled, wq[pl.ds(first, half), :], preferred_element_type=f32
            )
            acc[:, q_cols:] += jnp.dot(
                scaled, wkv[pl.ds(first, half), :], preferred_element_type=f32
            )
        return carry

    lax.fori_loop(0, n, project, 0)

    scale = lax.rsqrt(sumsq[...] * (1.0 / (width * n)) + 1e-05)
    cosine, sine = cos_ref[...], sin_ref[...]

    def rotary(v):
        return v * cosine + pltpu.roll(v, HEAD_SIZE // 2, 1) * sine

    for h in range(heads_here):
        d, hh = h // half_heads, h % half_heads
        v = acc[:, h * HEAD_SIZE : (h + 1) * HEAD_SIZE] * scale
        qbuf[d, 0, hh * tokens : (hh + 1) * tokens, :] = rotary(v).astype(bf16)

    def q_copy(d, s):
        return send(
            qbuf.at[d, s], qbuf.at[d, s + 1], q_send.at[d, s], q_recv.at[d, s + 1], d
        )

    def q_arrival(d, s):
        return send(qbuf.at[d, s - 1], qbuf.at[d, s], q_send.at[d, s], q_recv.at[d, s], d)

    def kv_copy(d, s):
        return send(
            kvbuf.at[d, s], kvbuf.at[d, s + 1], kv_send.at[d, s], kv_recv.at[d, s + 1], d
        )

    def kv_arrival(d, s):
        return send(kvbuf.at[d, s - 1], kvbuf.at[d, s], kv_send.at[d, s], kv_recv.at[d, s], d)

    def after(s):
        return lax.rem(s + 1, n)

    def o_between(d, s, t, c):
        return (
            send(obuf.at[d, s, c], obuf.at[d, t, c], o_send.at[d, s, c], o_recv.at[d, t, c], d),
            send(
                mlbuf.at[d, s, c], mlbuf.at[d, t, c], ml_send.at[d, s, c], ml_recv.at[d, t, c], d
            ),
        )

    def o_copies(d, s, c):
        return o_between(d, s, after(s), c)

    def o_arrivals(d, t, c):
        return o_between(d, lax.rem(t + n - 1, n), t, c)

    chunk = half_heads // 2

    for d in range(2):
        q_copy(d, 0).start()
    is_key = jnp.broadcast_to(me * kv_cols, (tokens, HEAD_SIZE)) < key_cols
    for d in range(2):
        for c in range(kv_half // HEAD_SIZE):
            a = q_cols + d * kv_half + c * HEAD_SIZE
            v = (acc[:, a : a + HEAD_SIZE] * scale).astype(bf16).astype(f32)
            turned = jnp.where(is_key, rotary(v), v)
            kvbuf[d, 0, :, c * HEAD_SIZE : (c + 1) * HEAD_SIZE] = turned.astype(bf16)
        kv_copy(d, 0).start()

    factor = HEAD_SIZE ** (-0.5) * LOG2E

    def merged(m1, l1, o1, m2, l2, o2):
        m = jnp.maximum(m1, m2)
        a, b = jnp.exp2(m1 - m), jnp.exp2(m2 - m)
        return m, l1 * a + l2 * b, o1 * a + o2 * b

    def partial(keys, values_t, q, bias):
        scores = lax.dot_general(
            keys, q, (((1,), (1,)), ((), ())), preferred_element_type=f32
        ) * factor + bias
        m = jnp.max(scores, axis=0, keepdims=True)
        p = jnp.exp2(scores - m)
        l = jnp.sum(p, axis=0, keepdims=True)
        o = jnp.dot(values_t, p.astype(bf16), preferred_element_type=f32)
        return m, l, o

    def attend(s, carry):
        for d in range(2):

            @pl.when(s > 0)
            def _():
                q_arrival(d, s).wait_recv()

            @pl.when((s > 0) & (s < n - 1))
            def _():
                q_copy(d, s).start()

        for d in range(2):

            @pl.when(s > 0)
            def _():
                kv_arrival(d, s).wait_recv()

            @pl.when((s > 0) & (s < n - 1))
            def _():
                kv_copy(d, s).start()

            owner = owner_at(d, s)
            col = pl.multiple_of(owner * kv_cols + d * kv_half, 128)
            fresh_ref[:, pl.ds(col, kv_half)] = kvbuf[d, s]

        parts = []
        for d in range(2):
            owner = owner_at(d, s)
            head = lax.div(owner * heads_here, group)
            first = pl.multiple_of(head * HEAD_SIZE, HEAD_SIZE)
            keys = cache[:, pl.ds(first, HEAD_SIZE)]
            values_t = vt[pl.ds(first, HEAD_SIZE), :]
            bias = bias_ref[...]
            parts.append(
                [
                    partial(keys, values_t, qbuf[d, s, r : r + tokens, :], bias)
                    for r in range(0, rows, tokens)
                ]
            )

        for c in range(2):
            for d in range(2):

                @pl.when(s > 1)
                def _():
                    for copy in o_arrivals(d, s, c):
                        copy.wait_recv()

                for k in range(chunk):
                    i = c * chunk + k
                    m, l, o = parts[d][i]
                    own_span = slice(i * tokens, (i + 1) * tokens)
                    span = slice(k * tokens, (k + 1) * tokens)

                    @pl.when(s == 0)
                    def _():
                        own_o[d, :, own_span] = o
                        own_ml[d, 0:1, own_span] = m
                        own_ml[d, 1:2, own_span] = l

                    @pl.when(s == 1)
                    def _():
                        obuf[d, s, c, :, span] = o.astype(bf16)
                        mlbuf[d, s, c, 0:1, span] = m
                        mlbuf[d, s, c, 1:2, span] = l

                    @pl.when(s > 1)
                    def _():
                        m3, l3, o3 = merged(
                            mlbuf[d, s, c, 0:1, span], mlbuf[d, s, c, 1:2, span],
                            obuf[d, s, c, :, span].astype(f32), m, l, o,
                        )
                        obuf[d, s, c, :, span] = o3.astype(bf16)
                        mlbuf[d, s, c, 0:1, span] = m3
                        mlbuf[d, s, c, 1:2, span] = l3

                @pl.when(s > 0)
                def _():
                    for copy in o_copies(d, s, c):
                        copy.start()

        return carry

    lax.fori_loop(0, n, attend, 0)

    head = lax.div(me * heads_here, group)
    first = pl.multiple_of(head * HEAD_SIZE, HEAD_SIZE)
    fresh_keys = fresh_ref[:, pl.ds(first, HEAD_SIZE)]
    fresh_values_t = fresh_ref[
        :, pl.ds(pl.multiple_of(first + key_cols, HEAD_SIZE), HEAD_SIZE)
    ].T
    key_at = lax.broadcasted_iota(jnp.int32, (tokens, tokens), 0)
    query_at = lax.broadcasted_iota(jnp.int32, (tokens, tokens), 1)
    causal = jnp.where(key_at <= query_at, 0.0, NEG_FILL)
    for d in range(2):
        own_parts = []
        for i in range(half_heads):
            span = slice(i * tokens, (i + 1) * tokens)
            m, l, o = partial(fresh_keys, fresh_values_t, qbuf[d, 0, span, :], causal)
            own_parts.append(
                merged(own_ml[d, 0:1, span], own_ml[d, 1:2, span], own_o[d, :, span], m, l, o)
            )
        for c in range(2):
            for copy in o_arrivals(d, 0, c):
                copy.wait_recv()
        for i in range(half_heads):
            c, k = i // chunk, i % chunk
            span = slice(k * tokens, (k + 1) * tokens)
            _, l, o = merged(
                mlbuf[d, 0, c, 0:1, span], mlbuf[d, 0, c, 1:2, span],
                obuf[d, 0, c, :, span].astype(f32), *own_parts[i],
            )
            h = d * half_heads + i
            att[:, h * HEAD_SIZE : (h + 1) * HEAD_SIZE] = (o / l).T.astype(bf16)

    loads[3].wait()

    def r_between(d, s, t, c):
        span = pl.ds(c * piece, piece)
        return send(
            rbuf.at[d, s, span], rbuf.at[d, t, span], r_send.at[d, s, c], r_recv.at[d, t, c], d
        )

    def r_copy(d, s, c):
        return r_between(d, s, after(s), c)

    def r_arrival(d, t, c):
        return r_between(d, lax.rem(t + n - 1, n), t, c)

    def share(d, owner):
        col = pl.multiple_of(owner * width + d * half, 128)
        return jnp.dot(att[...], wo[:, pl.ds(col, half)], preferred_element_type=f32)

    def scatter(s, carry):
        parts = [share(d, owner_at(d, s)) for d in range(2)]
        for c in range(2):
            span = slice(c * piece, (c + 1) * piece)
            for d in range(2):

                @pl.when(s > 1)
                def _():
                    r_arrival(d, s, c).wait_recv()
                    rbuf[d, s, span] = (rbuf[d, s, span].astype(f32) + parts[d][span]).astype(bf16)

                @pl.when(s == 1)
                def _():
                    rbuf[d, s, span] = parts[d][span].astype(bf16)

                r_copy(d, s, c).start()
        return carry

    lax.fori_loop(1, n, scatter, 0)

    def cross(d):
        return pltpu.make_async_remote_copy(
            src_ref=upd.at[d], dst_ref=landed.at[d], send_sem=x_send.at[d],
            recv_sem=x_recv.at[d], device_id={"section": sec_next},
            device_id_type=pl.DeviceIdType.MESH,
        )

    mine = [own_ref[:, d * half : (d + 1) * half].astype(f32) + share(d, me) for d in range(2)]
    for d in range(2):
        for c in range(2):
            r_arrival(d, 0, c).wait_recv()
        upd[d] = (mine[d] + rbuf[d, 0].astype(f32)).astype(bf16)
        cross(d).start()
    for d in range(2):
        cross(d).wait_recv()
        handed_ref[:, d * half : (d + 1) * half] = landed[d]

    def sent(s, carry):
        for d in range(2):
            for c in range(2):
                h_copy(d, s, c).wait_send()
                r_copy(d, s + 1, c).wait_send()
                for copy in o_copies(d, s + 1, c):
                    copy.wait_send()
            q_copy(d, s).wait_send()
            kv_copy(d, s).wait_send()
        return carry

    lax.fori_loop(0, n - 1, sent, 0)
    for d in range(2):
        cross(d).wait_send()


def on_device(
    hidden, norm_gain, w_query, key_value_weight, w_out, cache_pages, prefix_len, page_owner
):
    n = lax.axis_size("tp")
    heads_here = QUERY_HEADS // n
    tokens, width = hidden.shape[1:]
    kv_cols = key_value_weight.shape[2]
    if heads_here % 4 or kv_cols % (2 * HEAD_SIZE) or KEY_VALUE_HEADS % (n // 2) or n % 2 or tokens % 32 or width % 256:
        return on_device_plain(
            hidden, norm_gain, w_query, key_value_weight, w_out, cache_pages, prefix_len,
            page_owner,
        )
    sections = lax.axis_size("section")
    me = lax.axis_index("tp")
    slots = cache_pages.shape[1]
    half, half_heads = width // 2, heads_here // 2
    rows = half_heads * tokens
    cached_len = prefix_len[0, 0]
    half_head = HEAD_SIZE // 2
    inv_freq = ROPE_BASE ** (-jnp.arange(half_head, dtype=jnp.float32) * (2.0 / HEAD_SIZE))
    places = (cached_len + jnp.arange(tokens, dtype=jnp.int32)).astype(jnp.float32)
    angles = places[:, None] * inv_freq[None, :]
    cosine, sine = jnp.cos(angles), jnp.sin(angles)
    cos2 = jnp.concatenate([cosine, cosine], axis=1)
    sin2 = jnp.concatenate([-sine, sine], axis=1)
    slot_at = me * slots + jnp.arange(slots, dtype=jnp.int32)
    bias = jnp.broadcast_to(
        jnp.where(slot_at < cached_len, 0.0, NEG_FILL).astype(jnp.float32)[:, None],
        (slots, tokens),
    )
    bf16, f32 = jnp.bfloat16, jnp.float32
    q_cols = heads_here * HEAD_SIZE
    full = norm_gain.shape[1]
    kv_all = kv_cols * n
    dma = pltpu.SemaphoreType.DMA
    handed, fresh_rot = pl.pallas_call(
        functools.partial(layer_kernel, n, sections, heads_here),
        out_shape=(
            jax.ShapeDtypeStruct((tokens, width), bf16),
            jax.ShapeDtypeStruct((tokens, kv_all), bf16),
        ),
        in_specs=[VMEM] * 5 + [ANY] * 4,
        out_specs=(VMEM, VMEM),
        scratch_shapes=[
            pltpu.VMEM((full, q_cols), bf16),
            pltpu.VMEM((full, kv_cols), bf16),
            pltpu.VMEM((q_cols, full), bf16),
            pltpu.VMEM((slots, kv_all), bf16),
            pltpu.VMEM((kv_all // 2, slots), bf16),
            pltpu.VMEM((2, n, tokens, half), bf16),
            pltpu.VMEM((tokens, q_cols + kv_cols), f32),
            pltpu.VMEM((tokens, 1), f32),
            pltpu.VMEM((2, n, rows, HEAD_SIZE), bf16),
            pltpu.VMEM((2, n, 2, HEAD_SIZE, rows // 2), bf16),
            pltpu.VMEM((2, n, 2, 2, rows // 2), f32),
            pltpu.VMEM((2, HEAD_SIZE, rows), f32),
            pltpu.VMEM((2, 8, rows), f32),
            pltpu.VMEM((2, n, tokens, kv_cols // 2), bf16),
            pltpu.VMEM((tokens, q_cols), bf16),
            pltpu.VMEM((2, n, tokens, half), bf16),
            pltpu.VMEM((2, tokens, half), bf16),
            pltpu.VMEM((2, tokens, half), bf16),
            dma((4,)),
        ]
        + [dma((2, n))] * 4
        + [dma((2, n, 2))] * 8
        + [dma((2,))] * 2,
        compiler_params=pltpu.CompilerParams(
            collective_id=0, has_side_effects=True, vmem_limit_bytes=VMEM_BYTES
        ),
    )(
        hidden[0], norm_gain, cos2, sin2, bias, w_query[0], key_value_weight[0], w_out[0],
        cache_pages[0],
    )
    picked, _, _ = fresh_pages(fresh_rot, page_owner[0], me)
    return (handed[None], picked.reshape(1, 1, MOST, PAGE, kv_all))


def solution(mesh):
    return jax.shard_map(
        on_device,
        mesh=mesh,
        in_specs=(
            P("section", "groups", "tp"),
            P("section", None),
            P("section", None, "tp"),
            P("section", None, "tp"),
            P("section", "tp", None),
            P("section", ("groups", "tp"), None),
            P("section", "groups"),
            P("section", "groups"),
        ),
        out_specs=(P("section", "groups", "tp"), P("section", "tp", "groups", None, None)),
        check_vma=False,
    )
```

```python
import functools

import jax
import jax.numpy as jnp
import numpy as np
from jax import lax
from jax.experimental import pallas as pl
from jax.experimental.pallas import tpu as pltpu
from jax.sharding import PartitionSpec as P

QUERY_HEADS = 64
KEY_VALUE_HEADS = 8
HEAD_SIZE = 128
SPAN_TOKENS = 128
PAGE = 8
MOST = 4
NPAGE = 16


ROPE_BASE = 500000.0
NEG_FILL = -1e30


def passed_along(array, axis, by):
    length = lax.axis_size(axis)
    return lax.ppermute(array, axis, [(i, (i + by) % length) for i in range(length)])


def apply_rotary(values, token_places):
    head_width = values.shape[-1]
    half_width = head_width // 2
    inv_freq = ROPE_BASE ** (-jnp.arange(half_width, dtype=jnp.float32) * (2.0 / head_width))
    angles = token_places.astype(jnp.float32)[:, None] * inv_freq[None, :]
    cosine = jnp.cos(angles)[:, None, :]
    sine_part = jnp.sin(angles)[:, None, :]
    first_half = values[..., :half_width]
    second_half = values[..., half_width:]
    return jnp.concatenate(
        [
            first_half * cosine - second_half * sine_part,
            second_half * cosine + first_half * sine_part,
        ],
        axis=-1,
    )


def rotate_fresh(new_key_value, token_places):
    key_column_count = KEY_VALUE_HEADS * HEAD_SIZE
    rotary_output = apply_rotary(
        new_key_value[:, :key_column_count]
        .astype(jnp.float32)
        .reshape(-1, KEY_VALUE_HEADS, HEAD_SIZE),
        token_places,
    )
    return jnp.concatenate(
        [
            rotary_output.reshape(-1, key_column_count).astype(jnp.bfloat16),
            new_key_value[:, key_column_count:],
        ],
        axis=1,
    )


def fresh_pages(fresh_rot, owners, my_index):
    page_index = jnp.arange(NPAGE, dtype=jnp.int32)
    same_owner = owners[:, None] == owners[None, :]
    earlier = page_index[None, :] < page_index[:, None]
    page_rank = jnp.sum((same_owner & earlier).astype(jnp.int32), axis=1)
    slot_index = jnp.arange(MOST, dtype=jnp.int32)
    matched = (owners[None, :] == my_index) & (page_rank[None, :] == slot_index[:, None])
    flat_pages = fresh_rot.reshape(NPAGE, PAGE * fresh_rot.shape[1])
    picked = jnp.dot(
        matched.astype(jnp.bfloat16), flat_pages, preferred_element_type=jnp.float32
    ).astype(jnp.bfloat16)
    slot_page = jnp.sum(jnp.where(matched, page_index[None, :], 0), axis=1)
    slot_live = jnp.any(matched, axis=1)
    return (picked, slot_page, slot_live)


def on_device_plain(
    hidden, norm_gain, w_query, key_value_weight, w_out, cache_pages, prefix_len, page_owner
):
    tp_size = lax.axis_size("tp")
    my_index = lax.axis_index("tp")
    heads_here = QUERY_HEADS // tp_size
    query_group_width = QUERY_HEADS // KEY_VALUE_HEADS
    key_column_count = KEY_VALUE_HEADS * HEAD_SIZE
    own_rows = hidden[0]
    full_rows = lax.all_gather(own_rows, "tp", axis=1, tiled=True)
    rows_f32 = full_rows.astype(jnp.float32)
    normed = (
        rows_f32
        * lax.rsqrt(jnp.mean(rows_f32 * rows_f32, axis=1, keepdims=True) + 1e-05)
        * norm_gain[0][None, :]
    ).astype(jnp.bfloat16)
    cached_len = prefix_len[0, 0]
    token_index = jnp.arange(SPAN_TOKENS, dtype=jnp.int32)
    token_places = cached_len + token_index
    query_f32 = jnp.dot(normed, w_query[0], preferred_element_type=jnp.float32).reshape(
        SPAN_TOKENS, heads_here, HEAD_SIZE
    )
    queries = (
        apply_rotary(query_f32, token_places)
        .astype(jnp.bfloat16)
        .reshape(SPAN_TOKENS, heads_here * HEAD_SIZE)
    )
    fresh_part = jnp.dot(normed, key_value_weight[0], preferred_element_type=jnp.float32).astype(
        jnp.bfloat16
    )
    cached = cache_pages[0]
    slots_here = cached.shape[0]
    head_table = np.arange(tp_size) * heads_here // query_group_width
    by_head = jnp.transpose(
        cached.reshape(slots_here, 2, KEY_VALUE_HEADS, HEAD_SIZE), (2, 0, 1, 3)
    ).reshape(KEY_VALUE_HEADS, slots_here, 2 * HEAD_SIZE)
    outgoing = jnp.stack([by_head[int(h)] for h in head_table])
    arrived = lax.all_to_all(outgoing, "tp", split_axis=0, concat_axis=0, tiled=True)
    fresh_all = lax.all_gather(fresh_part, "tp", axis=1, tiled=True)
    fresh_rot = rotate_fresh(fresh_all, token_places)
    picked, slot_page, slot_live = fresh_pages(fresh_rot, page_owner[0], my_index)
    kv_head = my_index * heads_here // query_group_width
    local_key_rows = lax.dynamic_slice_in_dim(fresh_rot, kv_head * HEAD_SIZE, HEAD_SIZE, 1)
    local_value_rows = lax.dynamic_slice_in_dim(
        fresh_rot, key_column_count + kv_head * HEAD_SIZE, HEAD_SIZE, 1
    )
    all_keys = jnp.concatenate(
        [arrived[:, :, :HEAD_SIZE].reshape(tp_size * slots_here, HEAD_SIZE), local_key_rows], axis=0
    )
    all_values = jnp.concatenate(
        [arrived[:, :, HEAD_SIZE:].reshape(tp_size * slots_here, HEAD_SIZE), local_value_rows],
        axis=0,
    )
    cache_mask = jnp.broadcast_to(
        (jnp.arange(tp_size * slots_here, dtype=jnp.int32) < cached_len)[None, :],
        (SPAN_TOKENS, tp_size * slots_here),
    )
    fresh_mask = token_index[None, :] <= token_index[:, None]
    visible_key_mask = jnp.concatenate([cache_mask, fresh_mask], axis=1)
    head_queries = queries.reshape(SPAN_TOKENS, heads_here, HEAD_SIZE)

    def per_query(head_slot):
        one_head = lax.dynamic_index_in_dim(head_queries, head_slot, 1, keepdims=False)
        scores = jnp.einsum(
            "td,kd->tk", one_head, all_keys, preferred_element_type=jnp.float32
        ) * HEAD_SIZE ** (-0.5)
        scores = jnp.where(visible_key_mask, scores, NEG_FILL)
        top_score = jnp.max(scores, axis=1, keepdims=True)
        weights = jnp.exp(scores - top_score)
        denominator = jnp.sum(weights, axis=1, keepdims=True)
        summed = jnp.dot(
            weights.astype(jnp.bfloat16), all_values, preferred_element_type=jnp.float32
        )
        return summed / denominator

    outputs = lax.map(per_query, jnp.arange(heads_here, dtype=jnp.int32))
    attended = (
        jnp.transpose(outputs, (1, 0, 2))
        .reshape(SPAN_TOKENS, heads_here * HEAD_SIZE)
        .astype(jnp.bfloat16)
    )
    out_weight = w_out[0]
    block_share = lax.psum_scatter(
        lax.dot_general(
            out_weight, attended, (((0,), (1,)), ((), ())), preferred_element_type=jnp.float32
        ).astype(jnp.bfloat16),
        "tp",
        scatter_dimension=0,
        tiled=True,
    ).astype(jnp.float32)
    updated = (own_rows.astype(jnp.float32) + block_share.T).astype(jnp.bfloat16)
    handed = passed_along(updated, "section", 1)
    return (handed[None], picked.reshape(1, 1, MOST, PAGE, 2 * key_column_count))


LOG2E = 1.4426950408889634
VMEM_BYTES = 60 * 1024 * 1024
ANY = pl.BlockSpec(memory_space=pl.ANY)
VMEM = pl.BlockSpec(memory_space=pltpu.VMEM)


def layer_kernel(
    n, sections, heads_here,
    own_ref, gain_ref, cos_ref, sin_ref, bias_ref, wq_hbm, wkv_hbm, wo_hbm, cache_hbm,
    handed_ref, fresh_ref,
    wq, wkv, wo, cache, vt, hbuf, acc, sumsq, qbuf, obuf, mlbuf, own_o, own_ml, kvbuf, att,
    rbuf, upd, landed,
    w_sem, q_send, q_recv, kv_send, kv_recv, o_send, o_recv, ml_send, ml_recv,
    h_send, h_recv, r_send, r_recv, x_send, x_recv,
):
    f32, bf16 = jnp.float32, jnp.bfloat16
    tokens, width = own_ref.shape
    half = width // 2
    half_heads = heads_here // 2
    q_cols = heads_here * HEAD_SIZE
    kv_cols = wkv.shape[1]
    kv_half = kv_cols // 2
    key_cols = KEY_VALUE_HEADS * HEAD_SIZE
    rows = half_heads * tokens
    wide = bias_ref.shape[1]
    group = QUERY_HEADS // KEY_VALUE_HEADS

    me = lax.axis_index("tp")
    z, y = lax.div(me, 2), lax.rem(me, 2)
    place = y * (n - 1 - z) + (1 - y) * z

    def at_place(p):
        p = lax.rem(p + 2 * n, n)
        c = lax.div(p, n // 2)
        return (1 - c) * (2 * p) + c * (2 * (n - 1 - p) + 1)

    to = (at_place(place + 1), at_place(place - 1))

    def owner_at(d, s):
        return at_place(place - s) if d == 0 else at_place(place + s)

    def send(src, dst, ssem, rsem, d):
        return pltpu.make_async_remote_copy(
            src_ref=src, dst_ref=dst, send_sem=ssem, recv_sem=rsem,
            device_id={"tp": to[d]}, device_id_type=pl.DeviceIdType.MESH,
        )

    loads = [
        pltpu.make_async_copy(src, dst, w_sem.at[i])
        for i, (src, dst) in enumerate(
            ((wq_hbm, wq), (wkv_hbm, wkv), (cache_hbm, cache), (wo_hbm, wo))
        )
    ]
    loads[0].start()
    loads[1].start()

    sec = lax.axis_index("section")
    sec_next = lax.rem(sec + 1, sections)
    sec_prev = lax.rem(sec + sections - 1, sections)
    barrier = pltpu.get_barrier_semaphore()
    for d in range(2):
        pl.semaphore_signal(
            barrier, inc=1, device_id={"tp": to[d]}, device_id_type=pl.DeviceIdType.MESH
        )
    pl.semaphore_signal(
        barrier, inc=1, device_id={"section": sec_prev}, device_id_type=pl.DeviceIdType.MESH
    )
    for d in range(2):
        hbuf[d, 0] = own_ref[:, d * half : (d + 1) * half]
    acc[...] = jnp.zeros_like(acc)
    sumsq[...] = jnp.zeros_like(sumsq)
    pl.semaphore_wait(barrier, 3)

    piece = tokens // 2

    def h_copy(d, s, c):
        span = pl.ds(c * piece, piece)
        return send(
            hbuf.at[d, s, span], hbuf.at[d, s + 1, span],
            h_send.at[d, s, c], h_recv.at[d, s + 1, c], d,
        )

    def h_arrival(d, s, c):
        span = pl.ds(c * piece, piece)
        return send(
            hbuf.at[d, s - 1, span], hbuf.at[d, s, span],
            h_send.at[d, s, c], h_recv.at[d, s, c], d,
        )

    turns = n // 2
    turn_heads = KEY_VALUE_HEADS // turns

    def project(s, carry):
        for c in range(2):
            for d in range(2):

                @pl.when(s > 0)
                def _():
                    h_arrival(d, s, c).wait_recv()

                @pl.when(s < n - 1)
                def _():
                    h_copy(d, s, c).start()

        @pl.when(s == n - turns)
        def _():
            loads[2].wait()

        @pl.when(s >= n - turns)
        def _():
            for k in range(turn_heads):
                g = (s - (n - turns)) * turn_heads + k
                a = pl.multiple_of(g * HEAD_SIZE, HEAD_SIZE)
                b = pl.multiple_of(g * HEAD_SIZE + key_cols, HEAD_SIZE)
                vt[pl.ds(a, HEAD_SIZE), :] = cache[:, pl.ds(b, HEAD_SIZE)].T

        @pl.when(s == 0)
        def _():
            loads[0].wait()
            loads[1].wait()
            loads[2].start()
            loads[3].start()

        for d in range(2):
            first = pl.multiple_of(owner_at(d, s) * width + d * half, 128)
            part = hbuf[d, s].astype(f32)
            sumsq[...] += jnp.sum(part * part, axis=1, keepdims=True)
            scaled = (part * gain_ref[:, pl.ds(first, half)]).astype(bf16)
            acc[:, :q_cols] += jnp.dot(
                scaled, wq[pl.ds(first, half), :], preferred_element_type=f32
            )
            acc[:, q_cols:] += jnp.dot(
                scaled, wkv[pl.ds(first, half), :], preferred_element_type=f32
            )
        return carry

    lax.fori_loop(0, n, project, 0)

    scale = lax.rsqrt(sumsq[...] * (1.0 / (width * n)) + 1e-05)
    cosine, sine = cos_ref[...], sin_ref[...]

    def rotary(v):
        return v * cosine + pltpu.roll(v, HEAD_SIZE // 2, 1) * sine

    for h in range(heads_here):
        d, hh = h // half_heads, h % half_heads
        v = acc[:, h * HEAD_SIZE : (h + 1) * HEAD_SIZE] * scale
        qbuf[d, 0, hh * tokens : (hh + 1) * tokens, :] = rotary(v).astype(bf16)

    def q_copy(d, s):
        return send(
            qbuf.at[d, s], qbuf.at[d, s + 1], q_send.at[d, s], q_recv.at[d, s + 1], d
        )

    def q_arrival(d, s):
        return send(qbuf.at[d, s - 1], qbuf.at[d, s], q_send.at[d, s], q_recv.at[d, s], d)

    def kv_copy(d, s):
        return send(
            kvbuf.at[d, s], kvbuf.at[d, s + 1], kv_send.at[d, s], kv_recv.at[d, s + 1], d
        )

    def kv_arrival(d, s):
        return send(kvbuf.at[d, s - 1], kvbuf.at[d, s], kv_send.at[d, s], kv_recv.at[d, s], d)

    def after(s):
        return lax.rem(s + 1, n)

    def o_copies(d, s):
        t = after(s)
        return (
            send(obuf.at[d, s], obuf.at[d, t], o_send.at[d, s], o_recv.at[d, t], d),
            send(mlbuf.at[d, s], mlbuf.at[d, t], ml_send.at[d, s], ml_recv.at[d, t], d),
        )

    def o_arrivals(d, t):
        s = lax.rem(t + n - 1, n)
        return (
            send(obuf.at[d, s], obuf.at[d, t], o_send.at[d, s], o_recv.at[d, t], d),
            send(mlbuf.at[d, s], mlbuf.at[d, t], ml_send.at[d, s], ml_recv.at[d, t], d),
        )

    for d in range(2):
        q_copy(d, 0).start()
    is_key = jnp.broadcast_to(me * kv_cols, (tokens, HEAD_SIZE)) < key_cols
    for d in range(2):
        for c in range(kv_half // HEAD_SIZE):
            a = q_cols + d * kv_half + c * HEAD_SIZE
            v = (acc[:, a : a + HEAD_SIZE] * scale).astype(bf16).astype(f32)
            turned = jnp.where(is_key, rotary(v), v)
            kvbuf[d, 0, :, c * HEAD_SIZE : (c + 1) * HEAD_SIZE] = turned.astype(bf16)
        kv_copy(d, 0).start()

    factor = HEAD_SIZE ** (-0.5) * LOG2E

    def merged(m1, l1, o1, m2, l2, o2):
        m = jnp.maximum(m1, m2)
        a, b = jnp.exp2(m1 - m), jnp.exp2(m2 - m)
        return m, l1 * a + l2 * b, o1 * a + o2 * b

    def partial(keys, values_t, q, bias):
        scores = lax.dot_general(
            keys, q, (((1,), (1,)), ((), ())), preferred_element_type=f32
        ) * factor + bias
        m = jnp.max(scores, axis=0, keepdims=True)
        p = jnp.exp2(scores - m)
        l = jnp.sum(p, axis=0, keepdims=True)
        o = jnp.dot(values_t, p.astype(bf16), preferred_element_type=f32)
        return m, l, o

    def attend(s, carry):
        for d in range(2):

            @pl.when(s > 0)
            def _():
                q_arrival(d, s).wait_recv()

            @pl.when((s > 0) & (s < n - 1))
            def _():
                q_copy(d, s).start()

        for d in range(2):

            @pl.when(s > 0)
            def _():
                kv_arrival(d, s).wait_recv()

            @pl.when((s > 0) & (s < n - 1))
            def _():
                kv_copy(d, s).start()

            owner = owner_at(d, s)
            col = pl.multiple_of(owner * kv_cols + d * kv_half, 128)
            fresh_ref[:, pl.ds(col, kv_half)] = kvbuf[d, s]

        for d in range(2):
            owner = owner_at(d, s)
            head = lax.div(owner * heads_here, group)
            first = pl.multiple_of(head * HEAD_SIZE, HEAD_SIZE)
            keys = cache[:, pl.ds(first, HEAD_SIZE)]
            values_t = vt[pl.ds(first, HEAD_SIZE), :]
            bias = bias_ref[...]
            parts = [
                partial(keys, values_t, qbuf[d, s, r : r + wide, :], bias)
                for r in range(0, rows, wide)
            ]

            @pl.when(s > 1)
            def _():
                for c in o_arrivals(d, s):
                    c.wait_recv()

            for i, (m, l, o) in enumerate(parts):
                span = slice(i * wide, (i + 1) * wide)

                @pl.when(s == 0)
                def _():
                    own_o[d, :, span] = o
                    own_ml[d, 0:1, span] = m
                    own_ml[d, 1:2, span] = l

                @pl.when(s == 1)
                def _():
                    obuf[d, s, :, span] = o.astype(bf16)
                    mlbuf[d, s, 0:1, span] = m
                    mlbuf[d, s, 1:2, span] = l

                @pl.when(s > 1)
                def _():
                    m3, l3, o3 = merged(
                        mlbuf[d, s, 0:1, span], mlbuf[d, s, 1:2, span],
                        obuf[d, s, :, span].astype(f32), m, l, o,
                    )
                    obuf[d, s, :, span] = o3.astype(bf16)
                    mlbuf[d, s, 0:1, span] = m3
                    mlbuf[d, s, 1:2, span] = l3

            @pl.when(s > 0)
            def _():
                for c in o_copies(d, s):
                    c.start()

        return carry

    lax.fori_loop(0, n, attend, 0)

    head = lax.div(me * heads_here, group)
    first = pl.multiple_of(head * HEAD_SIZE, HEAD_SIZE)
    fresh_keys = fresh_ref[:, pl.ds(first, HEAD_SIZE)]
    fresh_values_t = fresh_ref[
        :, pl.ds(pl.multiple_of(first + key_cols, HEAD_SIZE), HEAD_SIZE)
    ].T
    key_at = lax.broadcasted_iota(jnp.int32, (tokens, tokens), 0)
    query_at = lax.broadcasted_iota(jnp.int32, (tokens, tokens), 1)
    causal = jnp.where(key_at <= query_at, 0.0, NEG_FILL)
    for d in range(2):
        own_parts = []
        for i in range(half_heads):
            span = slice(i * tokens, (i + 1) * tokens)
            m, l, o = partial(fresh_keys, fresh_values_t, qbuf[d, 0, span, :], causal)
            own_parts.append(
                merged(own_ml[d, 0:1, span], own_ml[d, 1:2, span], own_o[d, :, span], m, l, o)
            )
        for c in o_arrivals(d, 0):
            c.wait_recv()
        for i in range(half_heads):
            span = slice(i * tokens, (i + 1) * tokens)
            _, l, o = merged(
                mlbuf[d, 0, 0:1, span], mlbuf[d, 0, 1:2, span],
                obuf[d, 0, :, span].astype(f32), *own_parts[i],
            )
            h = d * half_heads + i
            att[:, h * HEAD_SIZE : (h + 1) * HEAD_SIZE] = (o / l).T.astype(bf16)

    loads[3].wait()

    def r_between(d, s, t, c):
        span = pl.ds(c * piece, piece)
        return send(
            rbuf.at[d, s, span], rbuf.at[d, t, span], r_send.at[d, s, c], r_recv.at[d, t, c], d
        )

    def r_copy(d, s, c):
        return r_between(d, s, after(s), c)

    def r_arrival(d, t, c):
        return r_between(d, lax.rem(t + n - 1, n), t, c)

    def share(d, owner):
        col = pl.multiple_of(owner * width + d * half, 128)
        return jnp.dot(att[...], wo[:, pl.ds(col, half)], preferred_element_type=f32)

    def scatter(s, carry):
        parts = [share(d, owner_at(d, s)) for d in range(2)]
        for c in range(2):
            span = slice(c * piece, (c + 1) * piece)
            for d in range(2):

                @pl.when(s > 1)
                def _():
                    r_arrival(d, s, c).wait_recv()
                    rbuf[d, s, span] = (rbuf[d, s, span].astype(f32) + parts[d][span]).astype(bf16)

                @pl.when(s == 1)
                def _():
                    rbuf[d, s, span] = parts[d][span].astype(bf16)

                r_copy(d, s, c).start()
        return carry

    lax.fori_loop(1, n, scatter, 0)

    def cross(d):
        return pltpu.make_async_remote_copy(
            src_ref=upd.at[d], dst_ref=landed.at[d], send_sem=x_send.at[d],
            recv_sem=x_recv.at[d], device_id={"section": sec_next},
            device_id_type=pl.DeviceIdType.MESH,
        )

    mine = [own_ref[:, d * half : (d + 1) * half].astype(f32) + share(d, me) for d in range(2)]
    for d in range(2):
        for c in range(2):
            r_arrival(d, 0, c).wait_recv()
        upd[d] = (mine[d] + rbuf[d, 0].astype(f32)).astype(bf16)
        cross(d).start()
    for d in range(2):
        cross(d).wait_recv()
        handed_ref[:, d * half : (d + 1) * half] = landed[d]

    def sent(s, carry):
        for d in range(2):
            for c in range(2):
                h_copy(d, s, c).wait_send()
                r_copy(d, s + 1, c).wait_send()
            q_copy(d, s).wait_send()
            kv_copy(d, s).wait_send()
            for c in o_copies(d, s + 1):
                c.wait_send()
        return carry

    lax.fori_loop(0, n - 1, sent, 0)
    for d in range(2):
        cross(d).wait_send()


def on_device(
    hidden, norm_gain, w_query, key_value_weight, w_out, cache_pages, prefix_len, page_owner
):
    n = lax.axis_size("tp")
    heads_here = QUERY_HEADS // n
    tokens, width = hidden.shape[1:]
    kv_cols = key_value_weight.shape[2]
    if heads_here % 4 or kv_cols % (2 * HEAD_SIZE) or KEY_VALUE_HEADS % (n // 2) or n % 2 or tokens % 32 or width % 256:
        return on_device_plain(
            hidden, norm_gain, w_query, key_value_weight, w_out, cache_pages, prefix_len,
            page_owner,
        )
    sections = lax.axis_size("section")
    me = lax.axis_index("tp")
    slots = cache_pages.shape[1]
    half, half_heads = width // 2, heads_here // 2
    rows = half_heads * tokens
    cached_len = prefix_len[0, 0]
    half_head = HEAD_SIZE // 2
    inv_freq = ROPE_BASE ** (-jnp.arange(half_head, dtype=jnp.float32) * (2.0 / HEAD_SIZE))
    places = (cached_len + jnp.arange(tokens, dtype=jnp.int32)).astype(jnp.float32)
    angles = places[:, None] * inv_freq[None, :]
    cosine, sine = jnp.cos(angles), jnp.sin(angles)
    cos2 = jnp.concatenate([cosine, cosine], axis=1)
    sin2 = jnp.concatenate([-sine, sine], axis=1)
    slot_at = me * slots + jnp.arange(slots, dtype=jnp.int32)
    bias = jnp.broadcast_to(
        jnp.where(slot_at < cached_len, 0.0, NEG_FILL).astype(jnp.float32)[:, None],
        (slots, 2 * tokens),
    )
    bf16, f32 = jnp.bfloat16, jnp.float32
    q_cols = heads_here * HEAD_SIZE
    full = norm_gain.shape[1]
    kv_all = kv_cols * n
    dma = pltpu.SemaphoreType.DMA
    handed, fresh_rot = pl.pallas_call(
        functools.partial(layer_kernel, n, sections, heads_here),
        out_shape=(
            jax.ShapeDtypeStruct((tokens, width), bf16),
            jax.ShapeDtypeStruct((tokens, kv_all), bf16),
        ),
        in_specs=[VMEM] * 5 + [ANY] * 4,
        out_specs=(VMEM, VMEM),
        scratch_shapes=[
            pltpu.VMEM((full, q_cols), bf16),
            pltpu.VMEM((full, kv_cols), bf16),
            pltpu.VMEM((q_cols, full), bf16),
            pltpu.VMEM((slots, kv_all), bf16),
            pltpu.VMEM((kv_all // 2, slots), bf16),
            pltpu.VMEM((2, n, tokens, half), bf16),
            pltpu.VMEM((tokens, q_cols + kv_cols), f32),
            pltpu.VMEM((tokens, 1), f32),
            pltpu.VMEM((2, n, rows, HEAD_SIZE), bf16),
            pltpu.VMEM((2, n, HEAD_SIZE, rows), bf16),
            pltpu.VMEM((2, n, 2, rows), f32),
            pltpu.VMEM((2, HEAD_SIZE, rows), f32),
            pltpu.VMEM((2, 8, rows), f32),
            pltpu.VMEM((2, n, tokens, kv_cols // 2), bf16),
            pltpu.VMEM((tokens, q_cols), bf16),
            pltpu.VMEM((2, n, tokens, half), bf16),
            pltpu.VMEM((2, tokens, half), bf16),
            pltpu.VMEM((2, tokens, half), bf16),
            dma((4,)),
        ]
        + [dma((2, n))] * 8
        + [dma((2, n, 2))] * 4
        + [dma((2,))] * 2,
        compiler_params=pltpu.CompilerParams(
            collective_id=0, has_side_effects=True, vmem_limit_bytes=VMEM_BYTES
        ),
    )(
        hidden[0], norm_gain, cos2, sin2, bias, w_query[0], key_value_weight[0], w_out[0],
        cache_pages[0],
    )
    picked, _, _ = fresh_pages(fresh_rot, page_owner[0], me)
    return (handed[None], picked.reshape(1, 1, MOST, PAGE, kv_all))


def solution(mesh):
    return jax.shard_map(
        on_device,
        mesh=mesh,
        in_specs=(
            P("section", "groups", "tp"),
            P("section", None),
            P("section", None, "tp"),
            P("section", None, "tp"),
            P("section", "tp", None),
            P("section", ("groups", "tp"), None),
            P("section", "groups"),
            P("section", "groups"),
        ),
        out_specs=(P("section", "groups", "tp"), P("section", "tp", "groups", None, None)),
        check_vma=False,
    )
```

```python
import functools

import jax
import jax.numpy as jnp
import numpy as np
from jax import lax
from jax.experimental import pallas as pl
from jax.experimental.pallas import tpu as pltpu
from jax.sharding import PartitionSpec as P

QUERY_HEADS = 64
KEY_VALUE_HEADS = 8
HEAD_SIZE = 128
SPAN_TOKENS = 128
PAGE = 8
MOST = 4
NPAGE = 16


ROPE_BASE = 500000.0
NEG_FILL = -1e30


def passed_along(array, axis, by):
    length = lax.axis_size(axis)
    return lax.ppermute(array, axis, [(i, (i + by) % length) for i in range(length)])


def apply_rotary(values, token_places):
    head_width = values.shape[-1]
    half_width = head_width // 2
    inv_freq = ROPE_BASE ** (-jnp.arange(half_width, dtype=jnp.float32) * (2.0 / head_width))
    angles = token_places.astype(jnp.float32)[:, None] * inv_freq[None, :]
    cosine = jnp.cos(angles)[:, None, :]
    sine_part = jnp.sin(angles)[:, None, :]
    first_half = values[..., :half_width]
    second_half = values[..., half_width:]
    return jnp.concatenate(
        [
            first_half * cosine - second_half * sine_part,
            second_half * cosine + first_half * sine_part,
        ],
        axis=-1,
    )


def rotate_fresh(new_key_value, token_places):
    key_column_count = KEY_VALUE_HEADS * HEAD_SIZE
    rotary_output = apply_rotary(
        new_key_value[:, :key_column_count]
        .astype(jnp.float32)
        .reshape(-1, KEY_VALUE_HEADS, HEAD_SIZE),
        token_places,
    )
    return jnp.concatenate(
        [
            rotary_output.reshape(-1, key_column_count).astype(jnp.bfloat16),
            new_key_value[:, key_column_count:],
        ],
        axis=1,
    )


def fresh_pages(fresh_rot, owners, my_index):
    page_index = jnp.arange(NPAGE, dtype=jnp.int32)
    same_owner = owners[:, None] == owners[None, :]
    earlier = page_index[None, :] < page_index[:, None]
    page_rank = jnp.sum((same_owner & earlier).astype(jnp.int32), axis=1)
    slot_index = jnp.arange(MOST, dtype=jnp.int32)
    matched = (owners[None, :] == my_index) & (page_rank[None, :] == slot_index[:, None])
    flat_pages = fresh_rot.reshape(NPAGE, PAGE * fresh_rot.shape[1])
    picked = jnp.dot(
        matched.astype(jnp.bfloat16), flat_pages, preferred_element_type=jnp.float32
    ).astype(jnp.bfloat16)
    slot_page = jnp.sum(jnp.where(matched, page_index[None, :], 0), axis=1)
    slot_live = jnp.any(matched, axis=1)
    return (picked, slot_page, slot_live)


def on_device_plain(
    hidden, norm_gain, w_query, key_value_weight, w_out, cache_pages, prefix_len, page_owner
):
    tp_size = lax.axis_size("tp")
    my_index = lax.axis_index("tp")
    heads_here = QUERY_HEADS // tp_size
    query_group_width = QUERY_HEADS // KEY_VALUE_HEADS
    key_column_count = KEY_VALUE_HEADS * HEAD_SIZE
    own_rows = hidden[0]
    full_rows = lax.all_gather(own_rows, "tp", axis=1, tiled=True)
    rows_f32 = full_rows.astype(jnp.float32)
    normed = (
        rows_f32
        * lax.rsqrt(jnp.mean(rows_f32 * rows_f32, axis=1, keepdims=True) + 1e-05)
        * norm_gain[0][None, :]
    ).astype(jnp.bfloat16)
    cached_len = prefix_len[0, 0]
    token_index = jnp.arange(SPAN_TOKENS, dtype=jnp.int32)
    token_places = cached_len + token_index
    query_f32 = jnp.dot(normed, w_query[0], preferred_element_type=jnp.float32).reshape(
        SPAN_TOKENS, heads_here, HEAD_SIZE
    )
    queries = (
        apply_rotary(query_f32, token_places)
        .astype(jnp.bfloat16)
        .reshape(SPAN_TOKENS, heads_here * HEAD_SIZE)
    )
    fresh_part = jnp.dot(normed, key_value_weight[0], preferred_element_type=jnp.float32).astype(
        jnp.bfloat16
    )
    cached = cache_pages[0]
    slots_here = cached.shape[0]
    head_table = np.arange(tp_size) * heads_here // query_group_width
    by_head = jnp.transpose(
        cached.reshape(slots_here, 2, KEY_VALUE_HEADS, HEAD_SIZE), (2, 0, 1, 3)
    ).reshape(KEY_VALUE_HEADS, slots_here, 2 * HEAD_SIZE)
    outgoing = jnp.stack([by_head[int(h)] for h in head_table])
    arrived = lax.all_to_all(outgoing, "tp", split_axis=0, concat_axis=0, tiled=True)
    fresh_all = lax.all_gather(fresh_part, "tp", axis=1, tiled=True)
    fresh_rot = rotate_fresh(fresh_all, token_places)
    picked, slot_page, slot_live = fresh_pages(fresh_rot, page_owner[0], my_index)
    kv_head = my_index * heads_here // query_group_width
    local_key_rows = lax.dynamic_slice_in_dim(fresh_rot, kv_head * HEAD_SIZE, HEAD_SIZE, 1)
    local_value_rows = lax.dynamic_slice_in_dim(
        fresh_rot, key_column_count + kv_head * HEAD_SIZE, HEAD_SIZE, 1
    )
    all_keys = jnp.concatenate(
        [arrived[:, :, :HEAD_SIZE].reshape(tp_size * slots_here, HEAD_SIZE), local_key_rows], axis=0
    )
    all_values = jnp.concatenate(
        [arrived[:, :, HEAD_SIZE:].reshape(tp_size * slots_here, HEAD_SIZE), local_value_rows],
        axis=0,
    )
    cache_mask = jnp.broadcast_to(
        (jnp.arange(tp_size * slots_here, dtype=jnp.int32) < cached_len)[None, :],
        (SPAN_TOKENS, tp_size * slots_here),
    )
    fresh_mask = token_index[None, :] <= token_index[:, None]
    visible_key_mask = jnp.concatenate([cache_mask, fresh_mask], axis=1)
    head_queries = queries.reshape(SPAN_TOKENS, heads_here, HEAD_SIZE)

    def per_query(head_slot):
        one_head = lax.dynamic_index_in_dim(head_queries, head_slot, 1, keepdims=False)
        scores = jnp.einsum(
            "td,kd->tk", one_head, all_keys, preferred_element_type=jnp.float32
        ) * HEAD_SIZE ** (-0.5)
        scores = jnp.where(visible_key_mask, scores, NEG_FILL)
        top_score = jnp.max(scores, axis=1, keepdims=True)
        weights = jnp.exp(scores - top_score)
        denominator = jnp.sum(weights, axis=1, keepdims=True)
        summed = jnp.dot(
            weights.astype(jnp.bfloat16), all_values, preferred_element_type=jnp.float32
        )
        return summed / denominator

    outputs = lax.map(per_query, jnp.arange(heads_here, dtype=jnp.int32))
    attended = (
        jnp.transpose(outputs, (1, 0, 2))
        .reshape(SPAN_TOKENS, heads_here * HEAD_SIZE)
        .astype(jnp.bfloat16)
    )
    out_weight = w_out[0]
    block_share = lax.psum_scatter(
        lax.dot_general(
            out_weight, attended, (((0,), (1,)), ((), ())), preferred_element_type=jnp.float32
        ).astype(jnp.bfloat16),
        "tp",
        scatter_dimension=0,
        tiled=True,
    ).astype(jnp.float32)
    updated = (own_rows.astype(jnp.float32) + block_share.T).astype(jnp.bfloat16)
    handed = passed_along(updated, "section", 1)
    return (handed[None], picked.reshape(1, 1, MOST, PAGE, 2 * key_column_count))


LOG2E = 1.4426950408889634
VMEM_BYTES = 60 * 1024 * 1024
ANY = pl.BlockSpec(memory_space=pl.ANY)
VMEM = pl.BlockSpec(memory_space=pltpu.VMEM)


def layer_kernel(
    n, sections, heads_here,
    own_ref, gain_ref, cos_ref, sin_ref, bias_ref, wq_hbm, wkv_hbm, wo_hbm, cache_hbm,
    handed_ref, fresh_ref,
    wq, wkv, wo, cache, vt, hbuf, acc, sumsq, qbuf, obuf, mlbuf, own_o, own_ml, kvbuf, att,
    rbuf, upd, landed,
    w_sem, wq_sem, wkv_sem, q_send, q_recv, kv_send, kv_recv, o_send, o_recv, ml_send, ml_recv,
    h_send, h_recv, r_send, r_recv, x_send, x_recv,
):
    f32, bf16 = jnp.float32, jnp.bfloat16
    tokens, width = own_ref.shape
    half = width // 2
    half_heads = heads_here // 2
    q_cols = heads_here * HEAD_SIZE
    kv_cols = wkv.shape[1]
    kv_half = kv_cols // 2
    key_cols = KEY_VALUE_HEADS * HEAD_SIZE
    rows = half_heads * tokens
    group = QUERY_HEADS // KEY_VALUE_HEADS

    me = lax.axis_index("tp")
    z, y = lax.div(me, 2), lax.rem(me, 2)
    place = y * (n - 1 - z) + (1 - y) * z

    def at_place(p):
        p = lax.rem(p + 2 * n, n)
        c = lax.div(p, n // 2)
        return (1 - c) * (2 * p) + c * (2 * (n - 1 - p) + 1)

    to = (at_place(place + 1), at_place(place - 1))

    def owner_at(d, s):
        return at_place(place - s) if d == 0 else at_place(place + s)

    def send(src, dst, ssem, rsem, d):
        return pltpu.make_async_remote_copy(
            src_ref=src, dst_ref=dst, send_sem=ssem, recv_sem=rsem,
            device_id={"tp": to[d]}, device_id_type=pl.DeviceIdType.MESH,
        )

    loads = [
        pltpu.make_async_copy(src, dst, w_sem.at[i])
        for i, (src, dst) in enumerate(
            ((cache_hbm, cache), (wo_hbm, wo))
        )
    ]

    def weight_loads(d, s):
        span = pl.ds(pl.multiple_of(owner_at(d, s) * width + d * half, 128), half)
        return (
            pltpu.make_async_copy(wq_hbm.at[span], wq.at[span], wq_sem.at[d, s]),
            pltpu.make_async_copy(wkv_hbm.at[span], wkv.at[span], wkv_sem.at[d, s]),
        )

    def load_weights(s, carry):
        for d in range(2):
            for copy in weight_loads(d, s):
                copy.start()
        return carry

    lax.fori_loop(0, n, load_weights, 0)

    sec = lax.axis_index("section")
    sec_next = lax.rem(sec + 1, sections)
    sec_prev = lax.rem(sec + sections - 1, sections)
    barrier = pltpu.get_barrier_semaphore()
    for d in range(2):
        pl.semaphore_signal(
            barrier, inc=1, device_id={"tp": to[d]}, device_id_type=pl.DeviceIdType.MESH
        )
    pl.semaphore_signal(
        barrier, inc=1, device_id={"section": sec_prev}, device_id_type=pl.DeviceIdType.MESH
    )
    for d in range(2):
        hbuf[d, 0] = own_ref[:, d * half : (d + 1) * half]
    acc[...] = jnp.zeros_like(acc)
    sumsq[...] = jnp.zeros_like(sumsq)
    pl.semaphore_wait(barrier, 3)

    piece = tokens // 2

    def h_copy(d, s, c):
        span = pl.ds(c * piece, piece)
        return send(
            hbuf.at[d, s, span], hbuf.at[d, s + 1, span],
            h_send.at[d, s, c], h_recv.at[d, s + 1, c], d,
        )

    def h_arrival(d, s, c):
        span = pl.ds(c * piece, piece)
        return send(
            hbuf.at[d, s - 1, span], hbuf.at[d, s, span],
            h_send.at[d, s, c], h_recv.at[d, s, c], d,
        )

    turns = n // 2
    turn_heads = KEY_VALUE_HEADS // turns

    def project(s, carry):
        for c in range(2):
            for d in range(2):

                @pl.when(s > 0)
                def _():
                    h_arrival(d, s, c).wait_recv()

                @pl.when(s < n - 1)
                def _():
                    h_copy(d, s, c).start()

        @pl.when(s == n - turns)
        def _():
            loads[0].wait()

        @pl.when(s >= n - turns)
        def _():
            for k in range(turn_heads):
                g = (s - (n - turns)) * turn_heads + k
                a = pl.multiple_of(g * HEAD_SIZE, HEAD_SIZE)
                b = pl.multiple_of(g * HEAD_SIZE + key_cols, HEAD_SIZE)
                vt[pl.ds(a, HEAD_SIZE), :] = cache[:, pl.ds(b, HEAD_SIZE)].T

        @pl.when(s == 0)
        def _():
            loads[0].start()
            loads[1].start()

        for d in range(2):
            for copy in weight_loads(d, s):
                copy.wait()
            first = pl.multiple_of(owner_at(d, s) * width + d * half, 128)
            part = hbuf[d, s].astype(f32)
            sumsq[...] += jnp.sum(part * part, axis=1, keepdims=True)
            scaled = (part * gain_ref[:, pl.ds(first, half)]).astype(bf16)
            acc[:, :q_cols] += jnp.dot(
                scaled, wq[pl.ds(first, half), :], preferred_element_type=f32
            )
            acc[:, q_cols:] += jnp.dot(
                scaled, wkv[pl.ds(first, half), :], preferred_element_type=f32
            )
        return carry

    lax.fori_loop(0, n, project, 0)

    scale = lax.rsqrt(sumsq[...] * (1.0 / (width * n)) + 1e-05)
    cosine, sine = cos_ref[...], sin_ref[...]

    def rotary(v):
        return v * cosine + pltpu.roll(v, HEAD_SIZE // 2, 1) * sine

    for h in range(heads_here):
        d, hh = h // half_heads, h % half_heads
        v = acc[:, h * HEAD_SIZE : (h + 1) * HEAD_SIZE] * scale
        qbuf[d, 0, hh * tokens : (hh + 1) * tokens, :] = rotary(v).astype(bf16)

    def q_copy(d, s):
        return send(
            qbuf.at[d, s], qbuf.at[d, s + 1], q_send.at[d, s], q_recv.at[d, s + 1], d
        )

    def q_arrival(d, s):
        return send(qbuf.at[d, s - 1], qbuf.at[d, s], q_send.at[d, s], q_recv.at[d, s], d)

    def kv_copy(d, s):
        return send(
            kvbuf.at[d, s], kvbuf.at[d, s + 1], kv_send.at[d, s], kv_recv.at[d, s + 1], d
        )

    def kv_arrival(d, s):
        return send(kvbuf.at[d, s - 1], kvbuf.at[d, s], kv_send.at[d, s], kv_recv.at[d, s], d)

    def after(s):
        return lax.rem(s + 1, n)

    def o_copies(d, s):
        t = after(s)
        return (
            send(obuf.at[d, s], obuf.at[d, t], o_send.at[d, s], o_recv.at[d, t], d),
            send(mlbuf.at[d, s], mlbuf.at[d, t], ml_send.at[d, s], ml_recv.at[d, t], d),
        )

    def o_arrivals(d, t):
        s = lax.rem(t + n - 1, n)
        return (
            send(obuf.at[d, s], obuf.at[d, t], o_send.at[d, s], o_recv.at[d, t], d),
            send(mlbuf.at[d, s], mlbuf.at[d, t], ml_send.at[d, s], ml_recv.at[d, t], d),
        )

    for d in range(2):
        q_copy(d, 0).start()
    is_key = jnp.broadcast_to(me * kv_cols, (tokens, HEAD_SIZE)) < key_cols
    for d in range(2):
        for c in range(kv_half // HEAD_SIZE):
            a = q_cols + d * kv_half + c * HEAD_SIZE
            v = (acc[:, a : a + HEAD_SIZE] * scale).astype(bf16).astype(f32)
            turned = jnp.where(is_key, rotary(v), v)
            kvbuf[d, 0, :, c * HEAD_SIZE : (c + 1) * HEAD_SIZE] = turned.astype(bf16)
        kv_copy(d, 0).start()

    factor = HEAD_SIZE ** (-0.5) * LOG2E

    def merged(m1, l1, o1, m2, l2, o2):
        m = jnp.maximum(m1, m2)
        a, b = jnp.exp2(m1 - m), jnp.exp2(m2 - m)
        return m, l1 * a + l2 * b, o1 * a + o2 * b

    def partial(keys, values_t, q, bias):
        scores = lax.dot_general(
            keys, q, (((1,), (1,)), ((), ())), preferred_element_type=f32
        ) * factor + bias
        m = jnp.max(scores, axis=0, keepdims=True)
        p = jnp.exp2(scores - m)
        l = jnp.sum(p, axis=0, keepdims=True)
        o = jnp.dot(values_t, p.astype(bf16), preferred_element_type=f32)
        return m, l, o

    def attend(s, carry):
        for d in range(2):

            @pl.when(s > 0)
            def _():
                q_arrival(d, s).wait_recv()

            @pl.when((s > 0) & (s < n - 1))
            def _():
                q_copy(d, s).start()

        for d in range(2):

            @pl.when(s > 0)
            def _():
                kv_arrival(d, s).wait_recv()

            @pl.when((s > 0) & (s < n - 1))
            def _():
                kv_copy(d, s).start()

            owner = owner_at(d, s)
            col = pl.multiple_of(owner * kv_cols + d * kv_half, 128)
            fresh_ref[:, pl.ds(col, kv_half)] = kvbuf[d, s]

        for d in range(2):
            owner = owner_at(d, s)
            head = lax.div(owner * heads_here, group)
            first = pl.multiple_of(head * HEAD_SIZE, HEAD_SIZE)
            keys = cache[:, pl.ds(first, HEAD_SIZE)]
            values_t = vt[pl.ds(first, HEAD_SIZE), :]
            bias = bias_ref[...]
            parts = [
                partial(keys, values_t, qbuf[d, s, r : r + tokens, :], bias)
                for r in range(0, rows, tokens)
            ]

            @pl.when(s > 1)
            def _():
                for c in o_arrivals(d, s):
                    c.wait_recv()

            for i, (m, l, o) in enumerate(parts):
                span = slice(i * tokens, (i + 1) * tokens)

                @pl.when(s == 0)
                def _():
                    own_o[d, :, span] = o
                    own_ml[d, 0:1, span] = m
                    own_ml[d, 1:2, span] = l

                @pl.when(s == 1)
                def _():
                    obuf[d, s, :, span] = o.astype(bf16)
                    mlbuf[d, s, 0:1, span] = m
                    mlbuf[d, s, 1:2, span] = l

                @pl.when(s > 1)
                def _():
                    m3, l3, o3 = merged(
                        mlbuf[d, s, 0:1, span], mlbuf[d, s, 1:2, span],
                        obuf[d, s, :, span].astype(f32), m, l, o,
                    )
                    obuf[d, s, :, span] = o3.astype(bf16)
                    mlbuf[d, s, 0:1, span] = m3
                    mlbuf[d, s, 1:2, span] = l3

            @pl.when(s > 0)
            def _():
                for c in o_copies(d, s):
                    c.start()

        return carry

    lax.fori_loop(0, n, attend, 0)

    head = lax.div(me * heads_here, group)
    first = pl.multiple_of(head * HEAD_SIZE, HEAD_SIZE)
    fresh_keys = fresh_ref[:, pl.ds(first, HEAD_SIZE)]
    fresh_values_t = fresh_ref[
        :, pl.ds(pl.multiple_of(first + key_cols, HEAD_SIZE), HEAD_SIZE)
    ].T
    key_at = lax.broadcasted_iota(jnp.int32, (tokens, tokens), 0)
    query_at = lax.broadcasted_iota(jnp.int32, (tokens, tokens), 1)
    causal = jnp.where(key_at <= query_at, 0.0, NEG_FILL)
    for d in range(2):
        own_parts = []
        for i in range(half_heads):
            span = slice(i * tokens, (i + 1) * tokens)
            m, l, o = partial(fresh_keys, fresh_values_t, qbuf[d, 0, span, :], causal)
            own_parts.append(
                merged(own_ml[d, 0:1, span], own_ml[d, 1:2, span], own_o[d, :, span], m, l, o)
            )
        for c in o_arrivals(d, 0):
            c.wait_recv()
        for i in range(half_heads):
            span = slice(i * tokens, (i + 1) * tokens)
            _, l, o = merged(
                mlbuf[d, 0, 0:1, span], mlbuf[d, 0, 1:2, span],
                obuf[d, 0, :, span].astype(f32), *own_parts[i],
            )
            h = d * half_heads + i
            att[:, h * HEAD_SIZE : (h + 1) * HEAD_SIZE] = (o / l).T.astype(bf16)

    loads[1].wait()

    def r_between(d, s, t, c):
        span = pl.ds(c * piece, piece)
        return send(
            rbuf.at[d, s, span], rbuf.at[d, t, span], r_send.at[d, s, c], r_recv.at[d, t, c], d
        )

    def r_copy(d, s, c):
        return r_between(d, s, after(s), c)

    def r_arrival(d, t, c):
        return r_between(d, lax.rem(t + n - 1, n), t, c)

    def share(d, owner):
        col = pl.multiple_of(owner * width + d * half, 128)
        return jnp.dot(att[...], wo[:, pl.ds(col, half)], preferred_element_type=f32)

    def scatter(s, carry):
        parts = [share(d, owner_at(d, s)) for d in range(2)]
        for c in range(2):
            span = slice(c * piece, (c + 1) * piece)
            for d in range(2):

                @pl.when(s > 1)
                def _():
                    r_arrival(d, s, c).wait_recv()
                    rbuf[d, s, span] = (rbuf[d, s, span].astype(f32) + parts[d][span]).astype(bf16)

                @pl.when(s == 1)
                def _():
                    rbuf[d, s, span] = parts[d][span].astype(bf16)

                r_copy(d, s, c).start()
        return carry

    lax.fori_loop(1, n, scatter, 0)

    def cross(d):
        return pltpu.make_async_remote_copy(
            src_ref=upd.at[d], dst_ref=landed.at[d], send_sem=x_send.at[d],
            recv_sem=x_recv.at[d], device_id={"section": sec_next},
            device_id_type=pl.DeviceIdType.MESH,
        )

    mine = [own_ref[:, d * half : (d + 1) * half].astype(f32) + share(d, me) for d in range(2)]
    for d in range(2):
        for c in range(2):
            r_arrival(d, 0, c).wait_recv()
        upd[d] = (mine[d] + rbuf[d, 0].astype(f32)).astype(bf16)
        cross(d).start()
    for d in range(2):
        cross(d).wait_recv()
        handed_ref[:, d * half : (d + 1) * half] = landed[d]

    def sent(s, carry):
        for d in range(2):
            for c in range(2):
                h_copy(d, s, c).wait_send()
                r_copy(d, s + 1, c).wait_send()
            q_copy(d, s).wait_send()
            kv_copy(d, s).wait_send()
            for c in o_copies(d, s + 1):
                c.wait_send()
        return carry

    lax.fori_loop(0, n - 1, sent, 0)
    for d in range(2):
        cross(d).wait_send()


def on_device(
    hidden, norm_gain, w_query, key_value_weight, w_out, cache_pages, prefix_len, page_owner
):
    n = lax.axis_size("tp")
    heads_here = QUERY_HEADS // n
    tokens, width = hidden.shape[1:]
    kv_cols = key_value_weight.shape[2]
    if heads_here % 2 or kv_cols % (2 * HEAD_SIZE) or KEY_VALUE_HEADS % (n // 2) or n % 2 or tokens % 32 or width % 256:
        return on_device_plain(
            hidden, norm_gain, w_query, key_value_weight, w_out, cache_pages, prefix_len,
            page_owner,
        )
    sections = lax.axis_size("section")
    me = lax.axis_index("tp")
    slots = cache_pages.shape[1]
    half, half_heads = width // 2, heads_here // 2
    rows = half_heads * tokens
    cached_len = prefix_len[0, 0]
    half_head = HEAD_SIZE // 2
    inv_freq = ROPE_BASE ** (-jnp.arange(half_head, dtype=jnp.float32) * (2.0 / HEAD_SIZE))
    places = (cached_len + jnp.arange(tokens, dtype=jnp.int32)).astype(jnp.float32)
    angles = places[:, None] * inv_freq[None, :]
    cosine, sine = jnp.cos(angles), jnp.sin(angles)
    cos2 = jnp.concatenate([cosine, cosine], axis=1)
    sin2 = jnp.concatenate([-sine, sine], axis=1)
    slot_at = me * slots + jnp.arange(slots, dtype=jnp.int32)
    bias = jnp.broadcast_to(
        jnp.where(slot_at < cached_len, 0.0, NEG_FILL).astype(jnp.float32)[:, None],
        (slots, tokens),
    )
    bf16, f32 = jnp.bfloat16, jnp.float32
    q_cols = heads_here * HEAD_SIZE
    full = norm_gain.shape[1]
    kv_all = kv_cols * n
    dma = pltpu.SemaphoreType.DMA
    handed, fresh_rot = pl.pallas_call(
        functools.partial(layer_kernel, n, sections, heads_here),
        out_shape=(
            jax.ShapeDtypeStruct((tokens, width), bf16),
            jax.ShapeDtypeStruct((tokens, kv_all), bf16),
        ),
        in_specs=[VMEM] * 5 + [ANY] * 4,
        out_specs=(VMEM, VMEM),
        scratch_shapes=[
            pltpu.VMEM((full, q_cols), bf16),
            pltpu.VMEM((full, kv_cols), bf16),
            pltpu.VMEM((q_cols, full), bf16),
            pltpu.VMEM((slots, kv_all), bf16),
            pltpu.VMEM((kv_all // 2, slots), bf16),
            pltpu.VMEM((2, n, tokens, half), bf16),
            pltpu.VMEM((tokens, q_cols + kv_cols), f32),
            pltpu.VMEM((tokens, 1), f32),
            pltpu.VMEM((2, n, rows, HEAD_SIZE), bf16),
            pltpu.VMEM((2, n, HEAD_SIZE, rows), bf16),
            pltpu.VMEM((2, n, 2, rows), f32),
            pltpu.VMEM((2, HEAD_SIZE, rows), f32),
            pltpu.VMEM((2, 8, rows), f32),
            pltpu.VMEM((2, n, tokens, kv_cols // 2), bf16),
            pltpu.VMEM((tokens, q_cols), bf16),
            pltpu.VMEM((2, n, tokens, half), bf16),
            pltpu.VMEM((2, tokens, half), bf16),
            pltpu.VMEM((2, tokens, half), bf16),
            dma((2,)),
        ]
        + [dma((2, n))] * 10
        + [dma((2, n, 2))] * 4
        + [dma((2,))] * 2,
        compiler_params=pltpu.CompilerParams(
            collective_id=0, has_side_effects=True, vmem_limit_bytes=VMEM_BYTES
        ),
    )(
        hidden[0], norm_gain, cos2, sin2, bias, w_query[0], key_value_weight[0], w_out[0],
        cache_pages[0],
    )
    picked, _, _ = fresh_pages(fresh_rot, page_owner[0], me)
    return (handed[None], picked.reshape(1, 1, MOST, PAGE, kv_all))


def solution(mesh):
    return jax.shard_map(
        on_device,
        mesh=mesh,
        in_specs=(
            P("section", "groups", "tp"),
            P("section", None),
            P("section", None, "tp"),
            P("section", None, "tp"),
            P("section", "tp", None),
            P("section", ("groups", "tp"), None),
            P("section", "groups"),
            P("section", "groups"),
        ),
        out_specs=(P("section", "groups", "tp"), P("section", "tp", "groups", None, None)),
        check_vma=False,
    )
```
